512 devices in a mesh: row: 4 (over y), col: 16 (over z_lo, core), layer: 8 (over z_hi, x).
Axes of the slice: x: 4, y: 4, z: 16 (z_hi: 2, z_lo: 8; z = z_hi * 8 + z_lo), core: 2. Of those that a mesh axis runs over, the one named last changes fastest.
Arguments:
- density: bfloat16 [512, 128, 2176], P(('row', 'col', 'layer')), as said below
- pattern: int32 [512, 17], P(('row', 'col', 'layer')), may hold values from 0 to 1, as said below
- keep_flags: int32 [512, 21], P(('row', 'col', 'layer')), may hold values from 0 to 1, as said below
Outputs:
- purified: float32 [512, 128, 2688], P(('row', 'col', 'layer'))
The draws below stay inside these ranges and needn't reach their ends.
Inputs may be any that keep to these rules, and one draw needn't show every extreme that they name: `pattern`: flag of block row i at offset o (column o + 8) equals that of block row i + o modulo 512 at offset -o; offset 0 is always 1. `keep_flags`: flag of block row i at offset o (column o + 10) equals that of block row i + o modulo 512 at offset -o; offset 0 is always 1. `density`: Symmetric: the block of row i at offset o is the transpose of the block of row i + o modulo 512 at offset -o.
All inputs are finite; a program needn't handle non-finite values.
Results may differ from the reference program's by a relative error of at most 0.002.
Values may be sent and summed in bfloat16 or wider, within the bound.
No kernel may reach another device: no remote copies, remote signals or barrier semaphores. Data moves between devices by JAX's collectives and lax.ppermute only.
A program may use at most 64 MiB of HBM per device.

```python
import math
import jax
import jax.numpy as jnp
from jax import lax

BLK = 128
BAND_HALF = 8
KEEP_HALF = 10
SLOTS = 17
KEPT = 21
NB = 512


def mirror_flags(key, half, odds):
    slots = 2 * half + 1
    draws = (jax.random.randint(key, (NB, slots), 0, odds) != 0).astype(jnp.int32)
    offsets = jnp.arange(slots, dtype=jnp.int32) - half
    partner_rows = (jnp.arange(NB, dtype=jnp.int32)[:, None] + offsets[None, :]) % NB
    partner_slots = jnp.broadcast_to((slots - 1 - jnp.arange(slots, dtype=jnp.int32))[None, :], (NB, slots))
    mirrored = draws[partner_rows, partner_slots]
    return jnp.where(offsets[None, :] > 0, draws, jnp.where(offsets[None, :] < 0, mirrored, 1)).astype(jnp.int32)


def draw_density(key, part):
    key = jax.random.fold_in(key, 11)
    scale = 0.8 * (BLK * SLOTS) ** (-0.25)
    raw = jax.random.normal(key, (NB, SLOTS, BLK, BLK), jnp.float32)
    offsets = jnp.arange(SLOTS, dtype=jnp.int32) - BAND_HALF
    partner_rows = (jnp.arange(NB, dtype=jnp.int32)[:, None] + offsets[None, :]) % NB
    partner_slots = jnp.broadcast_to((SLOTS - 1 - jnp.arange(SLOTS, dtype=jnp.int32))[None, :], (NB, SLOTS))
    partner = raw[partner_rows, partner_slots]
    blocks = (raw + jnp.swapaxes(partner, 2, 3)) * (0.70710678 * scale)
    return blocks.transpose(0, 2, 1, 3).reshape(NB, BLK, SLOTS * BLK).astype(jnp.bfloat16)


def draw_pattern(key, part):
    key = jax.random.fold_in(key, 23)
    return mirror_flags(key, BAND_HALF, 8)


def draw_keep_flags(key, part):
    key = jax.random.fold_in(key, 37)
    return mirror_flags(key, KEEP_HALF, 4)


def setup_inputs(seed: int = 0) -> dict:
    key_of = jax.random.split(jax.random.key(seed), 4)
    return {
        "density": draw_density(jax.random.fold_in(key_of[3], 71), 0),
        "pattern": draw_pattern(jax.random.fold_in(key_of[3], 71), 0),
        "keep_flags": draw_keep_flags(jax.random.fold_in(key_of[3], 71), 0),
    }


def widen_flags(flags, extent, dtype):
    grown = jnp.broadcast_to(flags.astype(dtype)[..., None], flags.shape + (extent,))
    return grown.reshape(flags.shape[:-1] + (flags.shape[-1] * extent,))


def purify_row(own_strip, fetch_row, keep_row):
    extent = own_strip.shape[0]
    kept_mask = widen_flags(keep_row, extent, jnp.float32)[None, :]
    square_slots = []
    for out_offset in range(-KEEP_HALF, KEEP_HALF + 1):
        lowest = max(-BAND_HALF, out_offset - BAND_HALF)
        highest = min(BAND_HALF, out_offset + BAND_HALF)
        left_part = own_strip[:, (lowest + BAND_HALF) * extent:(highest + BAND_HALF + 1) * extent]
        right_part = jnp.concatenate(
            [fetch_row(offset)[:, (out_offset - offset + BAND_HALF) * extent:(out_offset - offset + BAND_HALF + 1) * extent]
             for offset in range(lowest, highest + 1)], axis=0)
        square_slots.append(jnp.dot(left_part, right_part, preferred_element_type=jnp.float32))
    square = kept_mask * jnp.concatenate(square_slots, axis=1)
    rounded = square.astype(jnp.bfloat16)
    cube_slots = []
    for out_offset in range(-KEEP_HALF, KEEP_HALF + 1):
        lowest = max(-KEEP_HALF, out_offset - BAND_HALF)
        highest = min(KEEP_HALF, out_offset + BAND_HALF)
        left_part = rounded[:, (lowest + KEEP_HALF) * extent:(highest + KEEP_HALF + 1) * extent]
        right_part = jnp.concatenate(
            [fetch_row(offset)[:, (out_offset - offset + BAND_HALF) * extent:(out_offset - offset + BAND_HALF + 1) * extent]
             for offset in range(lowest, highest + 1)], axis=0)
        cube_slots.append(jnp.dot(left_part, right_part, preferred_element_type=jnp.float32))
    cube_part = kept_mask * jnp.concatenate(cube_slots, axis=1)
    return kept_mask * (3.0 * square - 2.0 * cube_part)


def reference(density, pattern, keep_flags):
    masked = density * widen_flags(pattern, BLK, jnp.bfloat16)[:, None, :]
    padded = jnp.concatenate([masked[NB - KEEP_HALF:], masked, masked[:KEEP_HALF]], axis=0)
    group = math.gcd(NB, 8)

    def one_row(row_index):
        window = lax.dynamic_slice_in_dim(padded, row_index, 2 * KEEP_HALF + 1, 0)
        keep_row = lax.dynamic_index_in_dim(keep_flags, row_index, 0, keepdims=False)

        def fetch_row(offset):
            return window[KEEP_HALF + offset]

        return purify_row(window[KEEP_HALF], fetch_row, keep_row)

    def one_group(group_index):
        starts = group_index * group + jnp.arange(group, dtype=jnp.int32)
        return jax.vmap(one_row)(starts)

    blocks = lax.map(one_group, jnp.arange(NB // group, dtype=jnp.int32))
    return blocks.reshape(NB, BLK, KEPT * BLK)
```

```python
import functools

import jax
import jax.numpy as jnp
import numpy as np
from jax import lax
from jax.experimental import pallas as pl
from jax.experimental.pallas import tpu as pltpu
from jax.sharding import Mesh, PartitionSpec as P

BLK = 128
BAND_HALF = 8
KEEP_HALF = 10
KEPT = 21
AXES = ("y", "zl", "c", "zh", "x")
UPPER = BAND_HALF + 1
DUMMY = KEPT * UPPER


def canonical(row, offset, n):
    return (row % n, offset) if offset >= 0 else ((row + offset) % n, -offset)


def own_lists(core, p):
    if core == 0:
        same = list(range(-p, 1)) + list(range(-8, -4 - p))
        same += {0: [8], 1: [7, 8], 2: [7, 8], 3: [7, 8]}[p]
    else:
        same = list(range(0, 4 - p)) + list(range(8 - p, 9))
        same += {0: [-6, -5], 1: [-6], 2: [], 3: []}[p]
    mixed = list(range(-p - 4, -p)) + list(range(4 - p, 8 - p))
    return same, mixed


def make_plan(ny, nzl):
    n = ny * nzl * 16

    def place(y, zl, c, zh, x):
        return (((y % ny) * nzl + zl) * 2 + c) * 8 + zh * 4 + x

    coords = [(y, zl, c, zh, x) for y in range(ny) for zl in range(nzl) for c in range(2) for zh in range(2) for x in range(4)]

    def ring(y, zl, zh, step):
        z = zh * nzl + zl
        y += 1 if (step == 1 and zl == nzl - 1) else -1 if (step == -1 and zl == 0) else 0
        z = (z + step) % (2 * nzl)
        return y, z % nzl, z // nzl

    need = [{((i - KEEP_HALF + u) % n, o): u * UPPER + o for u in range(KEPT) for o in range(UPPER) if u + o < KEPT} for i in range(n)]
    same_side, share = [], []
    for i, (y, zl, c, zh, x) in enumerate(coords):
        same, mixed = own_lists(c, x)
        same_side.append(same)
        share.append(same + mixed)
    k1 = max(map(len, same_side))
    k2 = max(map(len, share))
    pad = lambda seq, k, fill=None: list(seq) + [fill] * (k - len(seq))
    own = [[canonical(i, o, n) for o in range(-8, 9)] for i in range(n)]
    sent1 = [pad([canonical(i, o, n) for o in same_side[i]], k1) for i in range(n)]
    sent2 = [pad([canonical(i, o, n) for o in share[i]], k2) for i in range(n)]
    peer = lambda i, **kw: place(*[{**dict(zip(AXES, coords[i])), **kw}[a] for a in AXES])
    flip = lambda i, a: peer(i, **{a: 1 - coords[i][AXES.index(a)]})
    got2 = [sum([sent2[peer(i, x=q)] for q in range(4)], []) for i in range(n)]
    got3 = [sum([sent1[flip(peer(i, x=q), "zh")] for q in range(4)], []) for i in range(n)]
    got2c = [got2[flip(i, "c")] for i in range(n)]
    got3c = [got3[flip(i, "c")] for i in range(n)]
    pairs_seam, pairs_z, pairs_far = [], [], []
    for i, (y, zl, c, zh, x) in enumerate(coords):
        if (zl, c, zh) in ((0, 0, 0), (nzl - 1, 1, 1)):
            pairs_seam.append((i, flip(i, "zh")))
        y2, zl2, zh2 = ring(y, zl, zh, 1 if c else -1)
        pairs_z.append((i, place(y2, zl2, 1 - c, zh2, x)))
        pairs_far.append((i, place(y2, zl2, c, zh2, x)))
    known = [set(own[i] + got2[i] + got3[i] + got2c[i] + got3c[i]) for i in range(n)]
    gathered = [own[i] + got2[i] + got2c[i] + got3[i] + got3c[i] for i in range(n)]

    def choose(pairs, sources, limit=None):
        sends = [[] for _ in range(n)]
        for s, d in pairs:
            have = set(sources(s))
            sends[s] = [b for b in need[d] if b in have and b not in known[d]]
        k = max(map(len, sends))
        sends = [pad(q, k) for q in sends]
        got = [[None] * k for _ in range(n)]
        for s, d in pairs:
            got[d] = sends[s]
            known[d] |= set(sends[s])
        return k, sends, got

    ks, sent_s, got_s = choose(pairs_seam, lambda s: own[s] + got2[s])
    kz, sent_z, got_z = choose(pairs_z, lambda s: gathered[s])
    pairs_far = [(s, d) for s, d in pairs_far if set(need[d]) - known[d]]
    kf, sent_f, got_f = choose(pairs_far, lambda s: gathered[s])
    for i in range(n):
        assert not (set(need[i]) - known[i])

    def where(lists, sources):
        return np.array([[src.index(b) if b is not None else 0 for b in q] for q, src in zip(lists, sources)], np.int32)

    spots = np.full((n, sum(map(len, (own[0], got2[0], got2c[0], got3[0], got3c[0], got_s[0], got_z[0], got_f[0])))), DUMMY, np.int32)
    for i in range(n):
        seen = set()
        for k, b in enumerate(own[i] + got2[i] + got2c[i] + got3[i] + got3c[i] + got_s[i] + got_z[i] + got_f[i]):
            if b is not None and b in need[i] and b not in seen:
                seen.add(b)
                spots[i, k] = need[i][b]
    first = np.concatenate([where(sent1, own), where(sent2, own)], axis=1)
    return dict(
        n=n, k1=k1, k2=k2, ks=ks, kz=kz, kf=kf, first=first, spots=spots,
        seam=where(sent_s, [o + g for o, g in zip(own, got2)]),
        z=where([a + b for a, b in zip(sent_z, sent_f)], gathered), pairs_seam=pairs_seam, pairs_z=pairs_z, pairs_far=pairs_far,
        pairs_zh=[(i, flip(i, "zh")) for i in range(n)], pairs_c=[(i, flip(i, "c")) for i in range(n)],
    )


def vmem(*shape, dtype=jnp.bfloat16):
    return jax.ShapeDtypeStruct(shape, dtype)


def whole():
    return pl.BlockSpec(memory_space=pltpu.VMEM)


def scalars():
    return pl.BlockSpec(memory_space=pltpu.SMEM)


def call(kernel, outs, n_scalar, n_vector, scratch=()):
    return pl.pallas_call(
        kernel,
        out_shape=outs,
        in_specs=[scalars()] * n_scalar + [whole()] * n_vector,
        out_specs=jax.tree.map(lambda _: whole(), outs),
        scratch_shapes=scratch,
        compiler_params=pltpu.CompilerParams(vmem_limit_bytes=48 << 20),
    )


def first_kernel(k1, k2, table, pattern, strip, masked, own, send1, send2):
    for slot in range(2 * BAND_HALF + 1):
        cols = slice(slot * BLK, (slot + 1) * BLK)
        block = strip[0, :, cols] * pattern[0, slot].astype(jnp.bfloat16)
        masked[:, cols] = block
        own[slot] = block if slot >= BAND_HALF else block.T

    def pack1(k, carry):
        send1[k] = own[table[k]]
        return carry

    def pack2(k, carry):
        block = own[table[k1 + k]]
        for q in range(4):
            send2[q, k] = block
        return carry

    lax.fori_loop(0, k1, pack1, 0)
    lax.fori_loop(0, k2, pack2, 0)


def gather_kernel(n_sources, table, *refs):
    sources, outs = refs[:n_sources], refs[n_sources:]
    start = 0
    for out in outs:

        def pack(k, carry, out=out, start=start):
            at = table[start + k]
            low = 0
            for source in sources:
                count = source.shape[0]

                @pl.when((at >= low) & (at < low + count))
                def _(source=source, low=low):
                    out[k] = source[at - low]

                low += count
            return carry

        lax.fori_loop(0, out.shape[0], pack, 0)
        start += out.shape[0]


def product(left, first, pool, v):
    last = KEPT - 1 - first
    total = None
    low, high = max(first, v - BAND_HALF), min(last, v)
    if low <= high:
        right = jnp.concatenate([pool[u * UPPER + v - u] for u in range(low, high + 1)], axis=0)
        total = jnp.dot(left[:, (low - first) * BLK : (high - first + 1) * BLK], right, preferred_element_type=jnp.float32)
    low, high = max(first, v + 1), min(last, v + BAND_HALF)
    if low <= high:
        right = jnp.concatenate([pool[v * UPPER + u - v] for u in range(low, high + 1)], axis=1)
        part = lax.dot_general(
            left[:, (low - first) * BLK : (high - first + 1) * BLK], right,
            (((1,), (1,)), ((), ())), preferred_element_type=jnp.float32)
        total = part if total is None else total + part
    return total


def final_kernel(spots, keep, masked, *refs):
    *sources, out, pool, square, rounded = refs
    low = 0
    for source in sources:

        def place(k, carry, source=source, low=low):
            at = spots[low + k]

            @pl.when(at < DUMMY)
            def _():
                pool[at] = source[k]

            return carry

        lax.fori_loop(0, source.shape[0], place, 0)
        low += source.shape[0]
    for v in range(KEPT):
        cols = slice(v * BLK, (v + 1) * BLK)
        value = product(masked, KEEP_HALF - BAND_HALF, pool, v) * keep[0, v].astype(jnp.float32)
        square[:, cols] = value
        rounded[:, cols] = value.astype(jnp.bfloat16)
    for v in range(KEPT):
        cols = slice(v * BLK, (v + 1) * BLK)
        flag = keep[0, v].astype(jnp.float32)
        cube = flag * product(rounded, 0, pool, v)
        out[0, :, cols] = flag * (3.0 * square[:, cols] - 2.0 * cube)


def solution(mesh):
    ny, nzl = mesh.shape["row"], mesh.shape["col"] // 2
    plan = make_plan(ny, nzl)
    fine = Mesh(mesh.devices.reshape(ny, nzl, 2, 2, 4), AXES)
    k1, k2, ks, kz, kf = (plan[k] for k in ("k1", "k2", "ks", "kz", "kf"))
    tables = np.concatenate([plan["first"], plan["seam"], plan["z"], plan["spots"]], axis=1)
    cuts = np.cumsum([k1 + k2, ks, kz + kf])

    def body(density, pattern, keep):
        mine = lax.dynamic_index_in_dim(jnp.asarray(tables), lax.axis_index(AXES), 0, keepdims=False)
        t_first, t_seam, t_z, t_spots = jnp.split(mine, cuts)
        masked, own, send1, send2 = call(
            lambda *r: first_kernel(k1, k2, *r),
            (vmem(BLK, 17 * BLK), vmem(17, BLK, BLK), vmem(k1, BLK, BLK), vmem(4, k2, BLK, BLK)), 2, 1,
        )(t_first, pattern, density)
        got1 = lax.ppermute(send1, AXES, plan["pairs_zh"])
        got2 = lax.all_to_all(send2, "x", 0, 0).reshape(4 * k2, BLK, BLK)
        send3 = jnp.broadcast_to(got1, (4, k1, BLK, BLK))
        got3 = lax.all_to_all(send3, "x", 0, 0).reshape(4 * k1, BLK, BLK)
        got2c = lax.ppermute(got2, AXES, plan["pairs_c"])
        send_s = call(functools.partial(gather_kernel, 2), vmem(ks, BLK, BLK), 1, 2)(t_seam, own, got2)
        got_s = lax.ppermute(send_s, AXES, plan["pairs_seam"])
        got3c = lax.ppermute(got3, AXES, plan["pairs_c"])
        send_z, send_f = call(functools.partial(gather_kernel, 5), (vmem(kz, BLK, BLK), vmem(kf, BLK, BLK)), 1, 5)(t_z, own, got2, got2c, got3, got3c)
        got_z = lax.ppermute(send_z, AXES, plan["pairs_z"])
        got_f = lax.ppermute(send_f, AXES, plan["pairs_far"])
        return call(
            final_kernel, vmem(1, BLK, KEPT * BLK, dtype=jnp.float32), 2, 9,
            [
                pltpu.VMEM((DUMMY, BLK, BLK), jnp.bfloat16),
                pltpu.VMEM((BLK, KEPT * BLK), jnp.float32),
                pltpu.VMEM((BLK, KEPT * BLK), jnp.bfloat16),
            ],
        )(t_spots, keep, masked, own, got2, got2c, got3, got3c, got_s, got_z, got_f)

    return jax.shard_map(
        body,
        mesh=fine,
        in_specs=(P(AXES, None, None), P(AXES, None), P(AXES, None)),
        out_specs=P(AXES, None, None),
        check_vma=False,
    )
```

```python
import functools

import jax
import jax.numpy as jnp
import numpy as np
from jax import lax
from jax.experimental import pallas as pl
from jax.experimental.pallas import tpu as pltpu
from jax.sharding import Mesh, PartitionSpec as P

BLK = 128
BAND_HALF = 8
KEEP_HALF = 10
KEPT = 21
AXES = ("y", "zl", "c", "zh", "x")
UPPER = BAND_HALF + 1
DUMMY = KEPT * UPPER


def canonical(row, offset, n):
    return (row % n, offset) if offset >= 0 else ((row + offset) % n, -offset)


def own_lists(core, half, p):
    if core == 0:
        same = list(range(-p, 1)) + list(range(-8, -4 - p))
        same += ({0: [8], 1: [7, 8], 2: [6, 7], 3: [5, 6]} if half == 0 else {0: [8], 1: [7, 8], 2: [], 3: []})[p]
    else:
        same = list(range(0, 4 - p)) + list(range(8 - p, 9))
        same += ({0: [], 1: [], 2: [-8, -7], 3: [-8]} if half == 0 else {0: [-6, -5], 1: [-7, -6], 2: [-8, -7], 3: [-8]})[p]
    mixed = list(range(-p - 4, -p)) + list(range(4 - p, 8 - p))
    return same, mixed


def make_plan(ny, nzl):
    n = ny * nzl * 16

    def place(y, zl, c, zh, x):
        return (((y % ny) * nzl + zl) * 2 + c) * 8 + zh * 4 + x % 4

    coords = [(y, zl, c, zh, x) for y in range(ny) for zl in range(nzl) for c in range(2) for zh in range(2) for x in range(4)]

    def ring(y, zl, zh, step):
        z = zh * nzl + zl
        y += 1 if (step == 1 and zl == nzl - 1) else -1 if (step == -1 and zl == 0) else 0
        z = (z + step) % (2 * nzl)
        return y, z % nzl, z // nzl

    def pad(blocks, k):
        return list(blocks) + [None] * (k - len(blocks))

    need = [{((i - KEEP_HALF + u) % n, o): u * UPPER + o for u in range(KEPT) for o in range(UPPER) if u + o < KEPT} for i in range(n)]
    lists = [own_lists(c, zh, x) for y, zl, c, zh, x in coords]
    k1 = max(len(same) for same, _ in lists)
    k2 = max(len(same + mixed) for same, mixed in lists)
    own = [[canonical(i, o, n) for o in range(-8, 9)] for i in range(n)]
    sent1 = [pad([canonical(i, o, n) for o in same], k1) for i, (same, _) in enumerate(lists)]
    sent2 = [pad([canonical(i, o, n) for o in same + mixed], k2) for i, (same, mixed) in enumerate(lists)]
    moves = {}
    moves["zh"] = [(i, place(y, zl, c, 1 - zh, x)) for i, (y, zl, c, zh, x) in enumerate(coords)]
    moves["c"] = [(i, place(y, zl, 1 - c, zh, x)) for i, (y, zl, c, zh, x) in enumerate(coords)]
    for step in (1, 2, 3):
        moves[f"x{step}"] = [(i, place(y, zl, c, zh, x + step)) for i, (y, zl, c, zh, x) in enumerate(coords)]
    moves["seam"], moves["z"], moves["far"] = [], [], []
    for i, (y, zl, c, zh, x) in enumerate(coords):
        if (zl, c, zh) in ((0, 0, 0), (nzl - 1, 1, 1)):
            moves["seam"].append((i, place(y, zl, c, 1 - zh, x)))
        y2, zl2, zh2 = ring(y, zl, zh, 1 if c else -1)
        moves["z"].append((i, place(y2, zl2, 1 - c, zh2, x)))
        for step in (1, -1):
            y2, zl2, zh2 = ring(y, zl, zh, step)
            if (zh2 == 0 and x < 2 and step == 1) or (zh2 == 1 and x >= 2 and step == -1):
                moves["far"].append((i, place(y2, zl2, c, zh2, x)))

    def moved(sends, name):
        got = [[None] * len(sends[0]) for _ in range(n)]
        for s, d in moves[name]:
            got[d] = sends[s]
        return got

    def join(*parts):
        return [sum(row, []) for row in zip(*parts)]

    got1 = moved(sent1, "zh")
    got2 = [moved(sent2, f"x{s}") for s in (1, 2, 3)]
    got3 = [moved(got1, f"x{s}") for s in (1, 2, 3)]
    stock2 = join(own, *got2)
    stock3 = join(stock2, got1, *got3)
    got_c = moved(join(sent2, *got2, got1, *got3), "c")
    known = [set(row) for row in join(stock3, got_c)]

    def choose(name, stock):
        sends = [[] for _ in range(n)]
        for s, d in moves[name]:
            sends[s] = [b for b in need[d] if b not in known[d] and b in set(stock[s])]
        k = max(map(len, sends))
        sends = [pad(q, k) for q in sends]
        got = moved(sends, name)
        for d in range(n):
            known[d] |= set(got[d])
        return sends, got

    sent_s, got_s = choose("seam", stock2)
    sent_a, got_a = choose("z", stock2)
    sent_b, got_b = choose("z", stock3)
    sent_f, got_f = choose("far", stock3)
    assert all(set(need[d]) <= known[d] for d in range(n))

    def where(sends, stock):
        return np.array([[src.index(b) if b is not None else 0 for b in q] for q, src in zip(sends, stock)], np.int32)

    arrived = join(stock3, got_c, got_s, got_a, got_b, got_f)
    spots = np.full((n, len(arrived[0])), DUMMY, np.int32)
    for i in range(n):
        seen = set()
        for k, b in enumerate(arrived[i]):
            if b in need[i] and b not in seen:
                seen.add(b)
                spots[i, k] = need[i][b]
    parts = [where(sent1, own), where(sent2, own), where(sent_s, stock2), where(sent_a, stock2), where(sent_b, stock3), where(sent_f, stock3), spots]
    starts = np.cumsum([0] + [q.shape[1] for q in parts])
    return moves, np.concatenate(parts, axis=1), [q.shape[1] for q in parts], [int(q) for q in starts]


def vmem(*shape, dtype=jnp.bfloat16):
    return jax.ShapeDtypeStruct(shape, dtype)


def whole():
    return pl.BlockSpec(memory_space=pltpu.VMEM)


def scalars():
    return pl.BlockSpec(memory_space=pltpu.SMEM)


def call(kernel, outs, n_scalar, n_vector, scratch=()):
    return pl.pallas_call(
        kernel,
        out_shape=outs,
        in_specs=[scalars()] * n_scalar + [whole()] * n_vector,
        out_specs=jax.tree.map(lambda _: whole(), outs),
        scratch_shapes=scratch,
        compiler_params=pltpu.CompilerParams(vmem_limit_bytes=48 << 20),
    )


def first_kernel(start, table, pattern, strip, masked, own, send1, send2):
    for slot in range(2 * BAND_HALF + 1):
        cols = slice(slot * BLK, (slot + 1) * BLK)
        block = strip[0, :, cols] * pattern[0, slot].astype(jnp.bfloat16)
        masked[:, cols] = block
        own[slot] = block if slot >= BAND_HALF else block.T
    gather(start, table, [own], [send1, send2])


def gather(start, table, sources, outs):
    for out in outs:

        def pack(k, carry, out=out, start=start):
            at = table[start + k]
            low = 0
            for source in sources:
                count = source.shape[0]

                @pl.when((at >= low) & (at < low + count))
                def _(source=source, low=low):
                    out[k] = source[at - low]

                low += count
            return carry

        lax.fori_loop(0, out.shape[0], pack, 0)
        start += out.shape[0]


def concatenate(sources, out):
    low = 0
    for source in sources:
        out[low : low + source.shape[0]] = source[...]
        low += source.shape[0]


def second_kernel(start, table, own, x1, x2, x3, seam, z):
    gather(start, table, [own, x1, x2, x3], [seam, z])


def third_kernel(start, table, own, send2, x1, x2, x3, got1, w1, w2, w3, z, far, both):
    gather(start, table, [own, x1, x2, x3, got1, w1, w2, w3], [z, far])
    concatenate([send2, x1, x2, x3, got1, w1, w2, w3], both)


def product(left, first, pool, v):
    last = KEPT - 1 - first
    total = None
    low, high = max(first, v - BAND_HALF), min(last, v)
    if low <= high:
        right = jnp.concatenate([pool[u * UPPER + v - u] for u in range(low, high + 1)], axis=0)
        total = jnp.dot(left[:, (low - first) * BLK : (high - first + 1) * BLK], right, preferred_element_type=jnp.float32)
    low, high = max(first, v + 1), min(last, v + BAND_HALF)
    if low <= high:
        right = jnp.concatenate([pool[v * UPPER + u - v] for u in range(low, high + 1)], axis=1)
        part = lax.dot_general(
            left[:, (low - first) * BLK : (high - first + 1) * BLK], right,
            (((1,), (1,)), ((), ())), preferred_element_type=jnp.float32)
        total = part if total is None else total + part
    return total


def final_kernel(start, spots, keep, masked, *refs):
    *sources, out, pool, square, rounded = refs
    low = start
    for source in sources:

        def place(k, carry, source=source, low=low):
            at = spots[low + k]

            @pl.when(at < DUMMY)
            def _():
                pool[at] = source[k]

            return carry

        lax.fori_loop(0, source.shape[0], place, 0)
        low += source.shape[0]
    for v in range(KEPT):
        cols = slice(v * BLK, (v + 1) * BLK)
        value = product(masked, KEEP_HALF - BAND_HALF, pool, v) * keep[0, v].astype(jnp.float32)
        square[:, cols] = value
        rounded[:, cols] = value.astype(jnp.bfloat16)
    for v in range(KEPT):
        cols = slice(v * BLK, (v + 1) * BLK)
        flag = keep[0, v].astype(jnp.float32)
        cube = flag * product(rounded, 0, pool, v)
        out[0, :, cols] = flag * (3.0 * square[:, cols] - 2.0 * cube)


def solution(mesh):
    ny, nzl = mesh.shape["row"], mesh.shape["col"] // 2
    moves, tables, counts, starts = make_plan(ny, nzl)
    k1, k2, ks, ka, kb, kf, _ = counts
    fine = Mesh(mesh.devices.reshape(ny, nzl, 2, 2, 4), AXES)

    def send(array, name):
        return lax.ppermute(array, AXES, moves[name])

    def body(density, pattern, keep):
        table = lax.dynamic_index_in_dim(jnp.asarray(tables), lax.axis_index(AXES), 0, keepdims=False)
        masked, own, send1, send2 = call(
            functools.partial(first_kernel, starts[0]),
            (vmem(BLK, 17 * BLK), vmem(17, BLK, BLK), vmem(k1, BLK, BLK), vmem(k2, BLK, BLK)), 2, 1,
        )(table, pattern, density)
        x = [send(send2, f"x{step}") for step in (1, 3, 2)]
        x = [x[0], x[2], x[1]]
        got1 = send(send1, "zh")
        *x, got1 = lax.optimization_barrier((*x, got1))
        w = [send(got1, f"x{step}") for step in (1, 3, 2)]
        w = [w[0], w[2], w[1]]
        send_s, send_a = call(
            functools.partial(second_kernel, starts[2]), (vmem(ks, BLK, BLK), vmem(ka, BLK, BLK)), 1, 4,
        )(table, own, *x)
        got_s, got_a = send(send_s, "seam"), send(send_a, "z")
        w1, w2, w3, got_s = lax.optimization_barrier((*w, got_s))
        send_b, send_f, both = call(
            functools.partial(third_kernel, starts[4]),
            (vmem(kb, BLK, BLK), vmem(kf, BLK, BLK), vmem(4 * (k1 + k2), BLK, BLK)), 1, 9,
        )(table, own, send2, *x, got1, w1, w2, w3)
        got_b, got_f, got_c = send(send_b, "z"), send(send_f, "far"), send(both, "c")
        return call(
            functools.partial(final_kernel, starts[6]), vmem(1, BLK, KEPT * BLK, dtype=jnp.float32), 2, 14,
            [
                pltpu.VMEM((DUMMY, BLK, BLK), jnp.bfloat16),
                pltpu.VMEM((BLK, KEPT * BLK), jnp.float32),
                pltpu.VMEM((BLK, KEPT * BLK), jnp.bfloat16),
            ],
        )(table, keep, masked, own, *x, got1, w1, w2, w3, got_c, got_s, got_a, got_b, got_f)

    return jax.shard_map(
        body,
        mesh=fine,
        in_specs=(P(AXES, None, None), P(AXES, None), P(AXES, None)),
        out_specs=P(AXES, None, None),
        check_vma=False,
    )
```

```python
import functools

import jax
import jax.numpy as jnp
import numpy as np
from jax import lax
from jax.experimental import pallas as pl
from jax.experimental.pallas import tpu as pltpu
from jax.sharding import Mesh, PartitionSpec as P

BLK = 128
BAND_HALF = 8
KEEP_HALF = 10
KEPT = 21
AXES = ("y", "zl", "c", "zh", "x")
UPPER = BAND_HALF + 1
DUMMY = KEPT * UPPER


def canonical(row, offset, n):
    return (row % n, offset) if offset >= 0 else ((row + offset) % n, -offset)


def own_lists(lower, p):
    if lower:
        same = list(range(-p, 1)) + list(range(-8, -4 - p))
    else:
        same = list(range(0, 4 - p)) + list(range(8 - p, 9))
    return same, list(range(-p - 4, -p)) + list(range(4 - p, 8 - p))


def make_plan(ny, nzl):
    n = ny * nzl * 16

    def place(y, zl, c, zh, x):
        return (((y % ny) * nzl + zl) * 2 + c) * 8 + zh * 4 + x % 4

    coords = [(y, zl, c, zh, x) for y in range(ny) for zl in range(nzl) for c in range(2) for zh in range(2) for x in range(4)]

    def ring(y, zl, zh, step):
        z = zh * nzl + zl
        y += 1 if (step == 1 and zl == nzl - 1) else -1 if (step == -1 and zl == 0) else 0
        z = (z + step) % (2 * nzl)
        return y, z % nzl, z // nzl

    def pad(blocks, k):
        return list(blocks) + [None] * (k - len(blocks))

    need = [{((i - KEEP_HALF + u) % n, o): u * UPPER + o for u in range(KEPT) for o in range(UPPER) if u + o < KEPT} for i in range(n)]
    lists = [own_lists(zh == 0, x) for y, zl, c, zh, x in coords]
    over = [own_lists(zh == 1, x)[0] for y, zl, c, zh, x in coords]
    own = [[canonical(i, o, n) for o in range(-8, 9)] for i in range(n)]
    sent1 = [[canonical(i, o, n) for o in same] for i, same in enumerate(over)]
    sent2 = [[canonical(i, o, n) for o in same + mixed] for i, (same, mixed) in enumerate(lists)]
    moves = {}
    moves["zh"] = [(i, place(y, zl, c, 1 - zh, x)) for i, (y, zl, c, zh, x) in enumerate(coords)]
    moves["c"] = [(i, place(y, zl, 1 - c, zh, x)) for i, (y, zl, c, zh, x) in enumerate(coords)]
    for step in (1, 2, 3):
        moves[f"x{step}"] = [(i, place(y, zl, c, zh, x + step)) for i, (y, zl, c, zh, x) in enumerate(coords)]
    moves["seam"], moves["z"], moves["far"] = [], [], []
    for i, (y, zl, c, zh, x) in enumerate(coords):
        if (zl, c, zh) in ((0, 0, 0), (nzl - 1, 1, 1)):
            moves["seam"].append((i, place(y, zl, c, 1 - zh, x)))
        y2, zl2, zh2 = ring(y, zl, zh, 1 if c else -1)
        moves["z"].append((i, place(y2, zl2, 1 - c, zh2, x)))
        for step in (1, -1):
            y2, zl2, zh2 = ring(y, zl, zh, step)
            if (zh2 == 0 and x < 2 and step == 1) or (zh2 == 1 and x >= 2 and step == -1):
                moves["far"].append((i, place(y2, zl2, c, zh2, x)))

    def moved(sends, name):
        got = [[None] * len(sends[0]) for _ in range(n)]
        for s, d in moves[name]:
            got[d] = sends[s]
        return got

    def join(*parts):
        return [sum(row, []) for row in zip(*parts)]

    got1 = moved(sent1, "zh")
    got2 = [moved(sent2, f"x{s}") for s in (1, 2, 3)]
    got3 = [moved(got1, f"x{s}") for s in (1, 2, 3)]
    stock2 = join(own, *got2)
    stock3 = join(stock2, got1, *got3)
    got_c = moved(join(sent2, *got2, got1, *got3), "c")
    known = [set(row) for row in join(stock3, got_c)]

    def choose(name, stock):
        sends = [[] for _ in range(n)]
        for s, d in moves[name]:
            sends[s] = [b for b in need[d] if b not in known[d] and b in set(stock[s])]
        k = max(map(len, sends))
        sends = [pad(q, k) for q in sends]
        got = moved(sends, name)
        for d in range(n):
            known[d] |= set(got[d])
        return sends, got

    sent_s, got_s = choose("seam", stock2)
    sent_a, got_a = choose("z", stock2)
    sent_b, got_b = choose("z", stock3)
    sent_t, got_t = choose("seam", stock3)
    sent_f, got_f = choose("far", stock3)
    assert all(set(need[d]) <= known[d] for d in range(n))

    def where(sends, stock):
        return np.array([[src.index(b) if b is not None else 0 for b in q] for q, src in zip(sends, stock)], np.int32)

    arrived = join(stock3, got_c, got_s, got_a, got_b, got_t, got_f)
    spots = np.full((n, len(arrived[0])), DUMMY, np.int32)
    for i in range(n):
        seen = set()
        for k, b in enumerate(arrived[i]):
            if b in need[i] and b not in seen:
                seen.add(b)
                spots[i, k] = need[i][b]
    parts = [where(sent1, own), where(sent2, own), where(sent_s, stock2), where(sent_a, stock2), where(sent_b, stock3), where(sent_t, stock3), where(sent_f, stock3), spots]
    starts = np.cumsum([0] + [q.shape[1] for q in parts])
    return moves, np.concatenate(parts, axis=1), [q.shape[1] for q in parts], [int(q) for q in starts]


def vmem(*shape, dtype=jnp.bfloat16):
    return jax.ShapeDtypeStruct(shape, dtype)


def whole():
    return pl.BlockSpec(memory_space=pltpu.VMEM)


def scalars():
    return pl.BlockSpec(memory_space=pltpu.SMEM)


def call(kernel, outs, n_scalar, n_vector, scratch=(), mib=8):
    return pl.pallas_call(
        kernel,
        out_shape=outs,
        in_specs=[scalars()] * n_scalar + [whole()] * n_vector,
        out_specs=jax.tree.map(lambda _: whole(), outs),
        scratch_shapes=scratch,
        compiler_params=pltpu.CompilerParams(vmem_limit_bytes=mib << 20),
    )


def first_kernel(start, table, pattern, strip, masked, own, send1, send2):
    for slot in range(2 * BAND_HALF + 1):
        cols = slice(slot * BLK, (slot + 1) * BLK)
        block = strip[0, :, cols] * pattern[0, slot].astype(jnp.bfloat16)
        masked[:, cols] = block
        own[slot] = block if slot >= BAND_HALF else block.T
    gather(start, table, [own], [send1, send2])


def gather(start, table, sources, outs):
    for out in outs:

        def pack(k, carry, out=out, start=start):
            at = table[start + k]
            low = 0
            for source in sources:
                count = source.shape[0]

                @pl.when((at >= low) & (at < low + count))
                def _(source=source, low=low):
                    out[k] = source[at - low]

                low += count
            return carry

        lax.fori_loop(0, out.shape[0], pack, 0)
        start += out.shape[0]


def concatenate(sources, out):
    low = 0
    for source in sources:
        out[low : low + source.shape[0]] = source[...]
        low += source.shape[0]


def second_kernel(start, table, own, x1, x2, x3, seam, z):
    gather(start, table, [own, x1, x2, x3], [seam, z])


def third_kernel(start, table, own, send2, x1, x2, x3, got1, w1, w2, w3, z, seam, far, both):
    gather(start, table, [own, x1, x2, x3, got1, w1, w2, w3], [z, seam, far])
    concatenate([send2, x1, x2, x3, got1, w1, w2, w3], both)


def product(left, first, pool, v, width):
    last = KEPT - 1 - first
    blank = jnp.zeros((BLK, BLK), jnp.bfloat16)
    total = None
    for upper in (True, False):

        def block(u, col):
            row, offset = (u, col - u) if upper else (col, u - col)
            return pool[row * UPPER + offset] if (0 if upper else 1) <= offset <= BAND_HALF else blank

        low, high = (v - BAND_HALF, v + width - 1) if upper else (v + 1, v + width - 1 + BAND_HALF)
        low, high = max(first, low), min(last, high)
        if low > high:
            continue
        across = [
            jnp.concatenate([block(u, col) for u in range(low, high + 1)], axis=0 if upper else 1)
            for col in range(v, v + width)
        ]
        part = lax.dot_general(
            left[:, (low - first) * BLK : (high - first + 1) * BLK],
            jnp.concatenate(across, axis=1 if upper else 0),
            (((1,), (0 if upper else 1,)), ((), ())),
            preferred_element_type=jnp.float32,
        )
        total = part if total is None else total + part
    return total


def flags(keep, v, width):
    return jnp.concatenate([jnp.full((1, BLK), keep[0, v + j].astype(jnp.float32)) for j in range(width)], axis=1)


def final_kernel(start, spots, keep, masked, *refs):
    *sources, out, pool, square, rounded = refs
    low = start
    for source in sources:

        def place(k, carry, source=source, low=low):
            at = spots[low + k]

            @pl.when(at < DUMMY)
            def _():
                pool[at] = source[k]

            return carry

        lax.fori_loop(0, source.shape[0], place, 0)
        low += source.shape[0]
    groups = [(v, min(2, KEPT - v)) for v in range(0, KEPT, 2)]
    for v, width in groups:
        cols = slice(v * BLK, (v + width) * BLK)
        value = product(masked, KEEP_HALF - BAND_HALF, pool, v, width) * flags(keep, v, width)
        square[:, cols] = value
        rounded[:, cols] = value.astype(jnp.bfloat16)
    for v, width in groups:
        cols = slice(v * BLK, (v + width) * BLK)
        flag = flags(keep, v, width)
        cube = flag * product(rounded, 0, pool, v, width)
        out[0, :, cols] = flag * (3.0 * square[:, cols] - 2.0 * cube)


def solution(mesh):
    ny, nzl = mesh.shape["row"], mesh.shape["col"] // 2
    moves, tables, counts, starts = make_plan(ny, nzl)
    k1, k2, ks, ka, kb, kt, kf, _ = counts
    fine = Mesh(mesh.devices.reshape(ny, nzl, 2, 2, 4), AXES)

    def send(array, name):
        return lax.ppermute(array, AXES, moves[name])

    def body(density, pattern, keep):
        table = lax.dynamic_index_in_dim(jnp.asarray(tables), lax.axis_index(AXES), 0, keepdims=False)
        masked, own, send1, send2 = call(
            functools.partial(first_kernel, starts[0]),
            (vmem(BLK, 17 * BLK), vmem(17, BLK, BLK), vmem(k1, BLK, BLK), vmem(k2, BLK, BLK)), 2, 1,
        )(table, pattern, density)
        x = [send(send2, f"x{step}") for step in (1, 3, 2)]
        x = [x[0], x[2], x[1]]
        got1 = send(send1, "zh")
        *x, got1 = lax.optimization_barrier((*x, got1))
        w = [send(got1, f"x{step}") for step in (1, 3, 2)]
        w = [w[0], w[2], w[1]]
        send_s, send_a = call(
            functools.partial(second_kernel, starts[2]), (vmem(ks, BLK, BLK), vmem(ka, BLK, BLK)), 1, 4,
        )(table, own, *x)
        got_s, got_a = send(send_s, "seam"), send(send_a, "z")
        w1, w2, w3, got_s, got_a = lax.optimization_barrier((*w, got_s, got_a))
        send_b, send_t, send_f, both = call(
            functools.partial(third_kernel, starts[4]),
            (vmem(kb, BLK, BLK), vmem(kt, BLK, BLK), vmem(kf, BLK, BLK), vmem(4 * (k1 + k2), BLK, BLK)), 1, 9,
        )(table, own, send2, *x, got1, w1, w2, w3)
        got_b, got_t, got_f, got_c = send(send_b, "z"), send(send_t, "seam"), send(send_f, "far"), send(both, "c")
        return call(
            functools.partial(final_kernel, starts[7]), vmem(1, BLK, KEPT * BLK, dtype=jnp.float32), 2, 15,
            [
                pltpu.VMEM((DUMMY, BLK, BLK), jnp.bfloat16),
                pltpu.VMEM((BLK, KEPT * BLK), jnp.float32),
                pltpu.VMEM((BLK, KEPT * BLK), jnp.bfloat16),
            ], 24,
        )(table, keep, masked, own, *x, got1, w1, w2, w3, got_c, got_s, got_a, got_b, got_t, got_f)

    return jax.shard_map(
        body,
        mesh=fine,
        in_specs=(P(AXES, None, None), P(AXES, None), P(AXES, None)),
        out_specs=P(AXES, None, None),
        check_vma=False,
    )
```

```python
import functools

import jax
import jax.numpy as jnp
import numpy as np
from jax import lax
from jax.experimental import pallas as pl
from jax.experimental.pallas import tpu as pltpu
from jax.sharding import Mesh, PartitionSpec as P

BLK = 128
BAND_HALF = 8
KEEP_HALF = 10
KEPT = 21
AXES = ("y", "zl", "c", "zh", "x")
UPPER = BAND_HALF + 1
DUMMY = KEPT * UPPER


def canonical(row, offset, n):
    return (row % n, offset) if offset >= 0 else ((row + offset) % n, -offset)


def own_lists(lower, p):
    if lower:
        same = list(range(-p, 1)) + list(range(-8, -4 - p))
    else:
        same = list(range(0, 4 - p)) + list(range(8 - p, 9))
    return same, list(range(-p - 4, -p)) + list(range(4 - p, 8 - p))


def make_plan(ny, nzl):
    n = ny * nzl * 16

    def place(y, zl, c, zh, x):
        return (((y % ny) * nzl + zl) * 2 + c) * 8 + zh * 4 + x % 4

    coords = [(y, zl, c, zh, x) for y in range(ny) for zl in range(nzl) for c in range(2) for zh in range(2) for x in range(4)]

    def ring(y, zl, zh, step):
        z = zh * nzl + zl
        y += 1 if (step == 1 and zl == nzl - 1) else -1 if (step == -1 and zl == 0) else 0
        z = (z + step) % (2 * nzl)
        return y, z % nzl, z // nzl

    def pad(blocks, k):
        return list(blocks) + [None] * (k - len(blocks))

    need = [{((i - KEEP_HALF + u) % n, o): u * UPPER + o for u in range(KEPT) for o in range(UPPER) if u + o < KEPT} for i in range(n)]
    lists = [own_lists(zh == 0, x) for y, zl, c, zh, x in coords]
    over = [own_lists(zh == 1, x)[0] for y, zl, c, zh, x in coords]
    own = [[canonical(i, o, n) for o in range(-8, 9)] for i in range(n)]
    sent1 = [[canonical(i, o, n) for o in same] for i, same in enumerate(over)]
    sent2 = [[canonical(i, o, n) for o in same + mixed] for i, (same, mixed) in enumerate(lists)]
    moves = {}
    moves["zh"] = [(i, place(y, zl, c, 1 - zh, x)) for i, (y, zl, c, zh, x) in enumerate(coords)]
    moves["c"] = [(i, place(y, zl, 1 - c, zh, x)) for i, (y, zl, c, zh, x) in enumerate(coords)]
    for step in (1, 2, 3):
        moves[f"x{step}"] = [(i, place(y, zl, c, zh, x + step)) for i, (y, zl, c, zh, x) in enumerate(coords)]
    moves["seam"], moves["z"], moves["far"] = [], [], []
    for i, (y, zl, c, zh, x) in enumerate(coords):
        if (zl, c, zh) in ((0, 0, 0), (nzl - 1, 1, 1)):
            moves["seam"].append((i, place(y, zl, c, 1 - zh, x)))
        y2, zl2, zh2 = ring(y, zl, zh, 1 if c else -1)
        moves["z"].append((i, place(y2, zl2, 1 - c, zh2, x)))
        for step in (1, -1):
            y2, zl2, zh2 = ring(y, zl, zh, step)
            if (zh2 == 0 and x < 2 and step == 1) or (zh2 == 1 and x >= 2 and step == -1):
                moves["far"].append((i, place(y2, zl2, c, zh2, x)))

    def moved(sends, name):
        got = [[None] * len(sends[0]) for _ in range(n)]
        for s, d in moves[name]:
            got[d] = sends[s]
        return got

    def join(*parts):
        return [sum(row, []) for row in zip(*parts)]

    got1 = moved(sent1, "zh")
    got2 = [moved(sent2, f"x{s}") for s in (1, 2, 3)]
    got3 = [moved(got1, f"x{s}") for s in (1, 2, 3)]
    stock2 = join(own, *got2)
    stock3 = join(stock2, got1, *got3)
    got_c = moved(join(sent2, *got2), "c")
    got_d = moved(join(got1, *got3), "c")
    stock4 = join(stock3, got_c)
    known = [set(row) for row in join(stock4, got_d)]

    def choose(name, stock):
        sends = [[] for _ in range(n)]
        for s, d in moves[name]:
            sends[s] = [b for b in need[d] if b not in known[d] and b in set(stock[s])]
        k = max(map(len, sends))
        sends = [pad(q, k) for q in sends]
        got = moved(sends, name)
        for d in range(n):
            known[d] |= set(got[d])
        return sends, got

    sent_s, got_s = choose("seam", stock2)
    sent_a, got_a = choose("z", stock2)
    sent_b, got_b = choose("z", stock4)
    sent_t, got_t = choose("seam", stock4)
    sent_f, got_f = choose("far", stock4)
    assert all(set(need[d]) <= known[d] for d in range(n))

    def where(sends, stock):
        return np.array([[src.index(b) if b is not None else 0 for b in q] for q, src in zip(sends, stock)], np.int32)

    arrived = join(stock4, got_d, got_s, got_a, got_b, got_t, got_f)
    spots = np.full((n, len(arrived[0])), DUMMY, np.int32)
    for i in range(n):
        seen = set()
        for k, b in enumerate(arrived[i]):
            if b in need[i] and b not in seen:
                seen.add(b)
                spots[i, k] = need[i][b]
    parts = [where(sent1, own), where(sent2, own), where(sent_s, stock2), where(sent_a, stock2), where(sent_b, stock4), where(sent_t, stock4), where(sent_f, stock4), spots]
    starts = np.cumsum([0] + [q.shape[1] for q in parts])
    return moves, np.concatenate(parts, axis=1), [q.shape[1] for q in parts], [int(q) for q in starts]


def vmem(*shape, dtype=jnp.bfloat16):
    return jax.ShapeDtypeStruct(shape, dtype)


def whole():
    return pl.BlockSpec(memory_space=pltpu.VMEM)


def scalars():
    return pl.BlockSpec(memory_space=pltpu.SMEM)


def call(kernel, outs, n_scalar, n_vector, scratch=(), mib=8):
    return pl.pallas_call(
        kernel,
        out_shape=outs,
        in_specs=[scalars()] * n_scalar + [whole()] * n_vector,
        out_specs=jax.tree.map(lambda _: whole(), outs),
        scratch_shapes=scratch,
        compiler_params=pltpu.CompilerParams(vmem_limit_bytes=mib << 20),
    )


def first_kernel(start, table, pattern, strip, masked, own, send1, send2):
    for slot in range(2 * BAND_HALF + 1):
        cols = slice(slot * BLK, (slot + 1) * BLK)
        block = strip[0, :, cols] * pattern[0, slot].astype(jnp.bfloat16)
        masked[:, cols] = block
        own[slot] = block if slot >= BAND_HALF else block.T
    gather(start, table, [own], [send1, send2])


def gather(start, table, sources, outs):
    for out in outs:

        def pack(k, carry, out=out, start=start):
            at = table[start + k]
            low = 0
            for source in sources:
                count = source.shape[0]

                @pl.when((at >= low) & (at < low + count))
                def _(source=source, low=low):
                    out[k] = source[at - low]

                low += count
            return carry

        lax.fori_loop(0, out.shape[0], pack, 0)
        start += out.shape[0]


def concatenate(sources, out):
    low = 0
    for source in sources:
        out[low : low + source.shape[0]] = source[...]
        low += source.shape[0]


def second_kernel(start, table, own, send2, x1, x2, x3, seam, z, both):
    gather(start, table, [own, x1, x2, x3], [seam, z])
    concatenate([send2, x1, x2, x3], both)


def third_kernel(start, table, own, x1, x2, x3, got1, w1, w2, w3, got_c, z, seam, far, both):
    gather(start, table, [own, x1, x2, x3, got1, w1, w2, w3, got_c], [z, seam, far])
    concatenate([got1, w1, w2, w3], both)


def product(left, first, pool, v, width):
    last = KEPT - 1 - first
    blank = jnp.zeros((BLK, BLK), jnp.bfloat16)
    total = None
    for upper in (True, False):

        def block(u, col):
            row, offset = (u, col - u) if upper else (col, u - col)
            return pool[row * UPPER + offset] if (0 if upper else 1) <= offset <= BAND_HALF else blank

        low, high = (v - BAND_HALF, v + width - 1) if upper else (v + 1, v + width - 1 + BAND_HALF)
        low, high = max(first, low), min(last, high)
        if low > high:
            continue
        across = [
            jnp.concatenate([block(u, col) for u in range(low, high + 1)], axis=0 if upper else 1)
            for col in range(v, v + width)
        ]
        part = lax.dot_general(
            left[:, (low - first) * BLK : (high - first + 1) * BLK],
            jnp.concatenate(across, axis=1 if upper else 0),
            (((1,), (0 if upper else 1,)), ((), ())),
            preferred_element_type=jnp.float32,
        )
        total = part if total is None else total + part
    return total


def flags(keep, v, width):
    return jnp.concatenate([jnp.full((1, BLK), keep[0, v + j].astype(jnp.float32)) for j in range(width)], axis=1)


def final_kernel(start, spots, keep, masked, *refs):
    *sources, out, pool, square, rounded = refs
    low = start
    for source in sources:

        def place(k, carry, source=source, low=low):
            at = spots[low + k]

            @pl.when(at < DUMMY)
            def _():
                pool[at] = source[k]

            return carry

        lax.fori_loop(0, source.shape[0], place, 0)
        low += source.shape[0]
    groups = [(v, min(2, KEPT - v)) for v in range(0, KEPT, 2)]
    for v, width in groups:
        cols = slice(v * BLK, (v + width) * BLK)
        value = product(masked, KEEP_HALF - BAND_HALF, pool, v, width) * flags(keep, v, width)
        square[:, cols] = value
        rounded[:, cols] = value.astype(jnp.bfloat16)
    for v, width in groups:
        cols = slice(v * BLK, (v + width) * BLK)
        flag = flags(keep, v, width)
        cube = flag * product(rounded, 0, pool, v, width)
        out[0, :, cols] = flag * (3.0 * square[:, cols] - 2.0 * cube)


def solution(mesh):
    ny, nzl = mesh.shape["row"], mesh.shape["col"] // 2
    moves, tables, counts, starts = make_plan(ny, nzl)
    k1, k2, ks, ka, kb, kt, kf, _ = counts
    fine = Mesh(mesh.devices.reshape(ny, nzl, 2, 2, 4), AXES)

    def send(array, name):
        return lax.ppermute(array, AXES, moves[name])

    def body(density, pattern, keep):
        table = lax.dynamic_index_in_dim(jnp.asarray(tables), lax.axis_index(AXES), 0, keepdims=False)
        masked, own, send1, send2 = call(
            functools.partial(first_kernel, starts[0]),
            (vmem(BLK, 17 * BLK), vmem(17, BLK, BLK), vmem(k1, BLK, BLK), vmem(k2, BLK, BLK)), 2, 1,
        )(table, pattern, density)
        x = [send(send2, f"x{step}") for step in (1, 2, 3)]
        got1 = send(send1, "zh")
        send_s, send_a, both2 = call(
            functools.partial(second_kernel, starts[2]),
            (vmem(ks, BLK, BLK), vmem(ka, BLK, BLK), vmem(4 * k2, BLK, BLK)), 1, 5,
        )(table, own, send2, *x)
        got1, send_s, send_a, both2 = lax.optimization_barrier((got1, send_s, send_a, both2))
        got_s, got_a, got_c = send(send_s, "seam"), send(send_a, "z"), send(both2, "c")
        w = [send(got1, f"x{step}") for step in (1, 2, 3)]
        *w, got_a, got_c, got_s = lax.optimization_barrier((*w, got_a, got_c, got_s))
        send_b, send_t, send_f, both3 = call(
            functools.partial(third_kernel, starts[4]),
            (vmem(kb, BLK, BLK), vmem(kt, BLK, BLK), vmem(kf, BLK, BLK), vmem(4 * k1, BLK, BLK)), 1, 9,
        )(table, own, *x, got1, *w, got_c)
        got_b, got_t, got_f, got_d = send(send_b, "z"), send(send_t, "seam"), send(send_f, "far"), send(both3, "c")
        return call(
            functools.partial(final_kernel, starts[7]), vmem(1, BLK, KEPT * BLK, dtype=jnp.float32), 2, 16,
            [
                pltpu.VMEM((DUMMY, BLK, BLK), jnp.bfloat16),
                pltpu.VMEM((BLK, KEPT * BLK), jnp.float32),
                pltpu.VMEM((BLK, KEPT * BLK), jnp.bfloat16),
            ], 24,
        )(table, keep, masked, own, *x, got1, *w, got_c, got_d, got_s, got_a, got_b, got_t, got_f)

    return jax.shard_map(
        body,
        mesh=fine,
        in_specs=(P(AXES, None, None), P(AXES, None), P(AXES, None)),
        out_specs=P(AXES, None, None),
        check_vma=False,
    )
```

```python
import functools

import jax
import jax.numpy as jnp
import numpy as np
from jax import lax
from jax.experimental import pallas as pl
from jax.experimental.pallas import tpu as pltpu
from jax.sharding import Mesh, PartitionSpec as P

BLK = 128
BAND_HALF = 8
KEEP_HALF = 10
KEPT = 21
AXES = ("y", "zl", "c", "zh", "x")
UPPER = BAND_HALF + 1
DUMMY = KEPT * UPPER


def canonical(row, offset, n):
    return (row % n, offset) if offset >= 0 else ((row + offset) % n, -offset)


def own_lists(p):
    return list(range(0, 4 - p)) + list(range(8 - p, 9)), list(range(-p - 4, -p)) + list(range(4 - p, 8 - p))


def make_plan(ny, nzl):
    n = ny * nzl * 16

    def place(y, zl, c, zh, x):
        return (((y % ny) * nzl + zl) * 2 + c) * 8 + zh * 4 + x % 4

    coords = [(y, zl, c, zh, x) for y in range(ny) for zl in range(nzl) for c in range(2) for zh in range(2) for x in range(4)]

    def ring(y, zl, zh, step):
        z = zh * nzl + zl
        y += 1 if (step == 1 and zl == nzl - 1) else -1 if (step == -1 and zl == 0) else 0
        z = (z + step) % (2 * nzl)
        return y, z % nzl, z // nzl

    def pad(blocks, k):
        return list(blocks) + [None] * (k - len(blocks))

    need = [{((i - KEEP_HALF + u) % n, o): u * UPPER + o for u in range(KEPT) for o in range(UPPER) if u + o < KEPT} for i in range(n)]
    lists = [own_lists(x) for y, zl, c, zh, x in coords]
    own = [[canonical(i, o, n) for o in range(-8, 9)] for i in range(n)]
    sent1 = [[canonical(i, o, n) for o in same] for i, (same, _) in enumerate(lists)]
    sent2 = [[canonical(i, o, n) for o in same + mixed] for i, (same, mixed) in enumerate(lists)]
    moves = {}
    moves["zh"] = [(i, place(y, zl, c, 1 - zh, x)) for i, (y, zl, c, zh, x) in enumerate(coords)]
    moves["c"] = [(i, place(y, zl, 1 - c, zh, x)) for i, (y, zl, c, zh, x) in enumerate(coords)]
    for step in (1, 2, 3):
        moves[f"x{step}"] = [(i, place(y, zl, c, zh, x + step)) for i, (y, zl, c, zh, x) in enumerate(coords)]
    moves["seam"], moves["z"], moves["far"] = [], [], []
    for i, (y, zl, c, zh, x) in enumerate(coords):
        if (zl, c, zh) in ((0, 0, 0), (nzl - 1, 1, 1)):
            moves["seam"].append((i, place(y, zl, c, 1 - zh, x)))
        y2, zl2, zh2 = ring(y, zl, zh, 1 if c else -1)
        moves["z"].append((i, place(y2, zl2, 1 - c, zh2, x)))
        for step in (1, -1):
            y2, zl2, zh2 = ring(y, zl, zh, step)
            if (zh2 == 0 and x < 2 and step == 1) or (zh2 == 1 and x >= 2 and step == -1):
                moves["far"].append((i, place(y2, zl2, c, zh2, x)))

    def moved(sends, name):
        got = [[None] * len(sends[0]) for _ in range(n)]
        for s, d in moves[name]:
            got[d] = sends[s]
        return got

    def join(*parts):
        return [sum(row, []) for row in zip(*parts)]

    got1 = moved(sent1, "zh")
    got2 = [moved(sent2, f"x{s}") for s in (1, 2, 3)]
    got3 = [moved(got1, f"x{s}") for s in (1, 2, 3)]
    stock2 = join(own, *got2)
    stock3 = join(stock2, got1, *got3)
    got_c = moved(join(sent2, *got2), "c")
    got_d = moved(join(got1, *got3), "c")
    stock4 = join(stock3, got_c)
    known = [set(row) for row in join(stock4, got_d)]

    def choose(name, stock):
        sends = [[] for _ in range(n)]
        for s, d in moves[name]:
            sends[s] = [b for b in need[d] if b not in known[d] and b in set(stock[s])]
        k = max(map(len, sends))
        sends = [pad(q, k) for q in sends]
        got = moved(sends, name)
        for d in range(n):
            known[d] |= set(got[d])
        return sends, got

    sent_s, got_s = choose("seam", stock2)
    sent_a, got_a = choose("z", stock2)
    sent_b, got_b = choose("z", stock4)
    sent_f, got_f = choose("far", stock4)
    assert all(set(need[d]) <= known[d] for d in range(n))

    def where(sends, stock):
        return np.array([[src.index(b) if b is not None else 0 for b in q] for q, src in zip(sends, stock)], np.int32)

    arrived = join(stock4, got_s, got_a, got_d, got_b, got_f)
    spots = np.full((n, len(arrived[0])), DUMMY, np.int32)
    for i in range(n):
        seen = set()
        for k, b in enumerate(arrived[i]):
            if b in need[i] and b not in seen:
                seen.add(b)
                spots[i, k] = need[i][b]
    parts = [where(sent1, own), where(sent2, own), where(sent_s, stock2), where(sent_a, stock2), where(sent_b, stock4), where(sent_f, stock4), spots]
    starts = np.cumsum([0] + [q.shape[1] for q in parts])
    return moves, np.concatenate(parts, axis=1), [q.shape[1] for q in parts], [int(q) for q in starts]


def vmem(*shape, dtype=jnp.bfloat16):
    return jax.ShapeDtypeStruct(shape, dtype)


def whole():
    return pl.BlockSpec(memory_space=pltpu.VMEM)


def scalars():
    return pl.BlockSpec(memory_space=pltpu.SMEM)


def call(kernel, outs, n_scalar, n_vector, scratch=(), mib=8):
    return pl.pallas_call(
        kernel,
        out_shape=outs,
        in_specs=[scalars()] * n_scalar + [whole()] * n_vector,
        out_specs=jax.tree.map(lambda _: whole(), outs),
        scratch_shapes=scratch,
        compiler_params=pltpu.CompilerParams(vmem_limit_bytes=mib << 20),
    )


def first_kernel(start, table, pattern, strip, masked, own, send1, send2):
    for slot in range(2 * BAND_HALF + 1):
        cols = slice(slot * BLK, (slot + 1) * BLK)
        block = strip[0, :, cols] * pattern[0, slot].astype(jnp.bfloat16)
        masked[:, cols] = block
        own[slot] = block if slot >= BAND_HALF else block.T
    gather(start, table, [own], [send1, send2])


def gather(start, table, sources, outs):
    for out in outs:

        def pack(k, carry, out=out, start=start):
            at = table[start + k]
            low = 0
            for source in sources:
                count = source.shape[0]

                @pl.when((at >= low) & (at < low + count))
                def _(source=source, low=low):
                    out[k] = source[at - low]

                low += count
            return carry

        lax.fori_loop(0, out.shape[0], pack, 0)
        start += out.shape[0]


def concatenate(sources, out):
    low = 0
    for source in sources:
        out[low : low + source.shape[0]] = source[...]
        low += source.shape[0]


def second_kernel(start, table, own, send2, x1, x2, x3, seam, z, both):
    gather(start, table, [own, x1, x2, x3], [seam, z])
    concatenate([send2, x1, x2, x3], both)


def third_kernel(start, table, own, x1, x2, x3, got1, w1, w2, w3, got_c, z, far, both):
    gather(start, table, [own, x1, x2, x3, got1, w1, w2, w3, got_c], [z, far])
    concatenate([got1, w1, w2, w3], both)


def product(left, first, pool, v, width):
    last = KEPT - 1 - first
    blank = jnp.zeros((BLK, BLK), jnp.bfloat16)
    total = None
    for upper in (True, False):

        def block(u, col):
            row, offset = (u, col - u) if upper else (col, u - col)
            return pool[row * UPPER + offset] if (0 if upper else 1) <= offset <= BAND_HALF else blank

        low, high = (v - BAND_HALF, v + width - 1) if upper else (v + 1, v + width - 1 + BAND_HALF)
        low, high = max(first, low), min(last, high)
        if low > high:
            continue
        across = [
            jnp.concatenate([block(u, col) for u in range(low, high + 1)], axis=0 if upper else 1)
            for col in range(v, v + width)
        ]
        part = lax.dot_general(
            left[:, (low - first) * BLK : (high - first + 1) * BLK],
            jnp.concatenate(across, axis=1 if upper else 0),
            (((1,), (0 if upper else 1,)), ((), ())),
            preferred_element_type=jnp.float32,
        )
        total = part if total is None else total + part
    return total


def flags(keep, v, width):
    return jnp.concatenate([jnp.full((1, BLK), keep[0, v + j].astype(jnp.float32)) for j in range(width)], axis=1)


def place(low, spots, sources, pool):
    for source in sources:

        def put(k, carry, source=source, low=low):
            at = spots[low + k]

            @pl.when(at < DUMMY)
            def _():
                pool[at] = source[k]

            return carry

        lax.fori_loop(0, source.shape[0], put, 0)
        low += source.shape[0]


def early_kernel(start, spots, *refs):
    place(start, spots, refs[:-1], refs[-1])


def final_kernel(start, spots, keep, masked, *refs):
    *sources, _, out, pool, square, rounded = refs
    place(start, spots, sources, pool)
    groups = [(v, min(2, KEPT - v)) for v in range(0, KEPT, 2)]
    for v, width in groups:
        cols = slice(v * BLK, (v + width) * BLK)
        value = product(masked, KEEP_HALF - BAND_HALF, pool, v, width) * flags(keep, v, width)
        square[:, cols] = value
        rounded[:, cols] = value.astype(jnp.bfloat16)
    for v, width in groups:
        cols = slice(v * BLK, (v + width) * BLK)
        flag = flags(keep, v, width)
        cube = flag * product(rounded, 0, pool, v, width)
        out[0, :, cols] = flag * (3.0 * square[:, cols] - 2.0 * cube)


def solution(mesh):
    ny, nzl = mesh.shape["row"], mesh.shape["col"] // 2
    moves, tables, counts, starts = make_plan(ny, nzl)
    k1, k2, ks, ka, kb, kf, _ = counts
    fine = Mesh(mesh.devices.reshape(ny, nzl, 2, 2, 4), AXES)

    def send(array, name):
        return lax.ppermute(array, AXES, moves[name])

    def body(density, pattern, keep):
        table = lax.dynamic_index_in_dim(jnp.asarray(tables), lax.axis_index(AXES), 0, keepdims=False)
        masked, own, send1, send2 = call(
            functools.partial(first_kernel, starts[0]),
            (vmem(BLK, 17 * BLK), vmem(17, BLK, BLK), vmem(k1, BLK, BLK), vmem(k2, BLK, BLK)), 2, 1,
        )(table, pattern, density)
        x = [send(send2, f"x{step}") for step in (1, 2, 3)]
        got1 = send(send1, "zh")
        send_s, send_a, both2 = call(
            functools.partial(second_kernel, starts[2]),
            (vmem(ks, BLK, BLK), vmem(ka, BLK, BLK), vmem(4 * k2, BLK, BLK)), 1, 5,
        )(table, own, send2, *x)
        got1, send_s, send_a, both2 = lax.optimization_barrier((got1, send_s, send_a, both2))
        got_s, got_a, got_c = send(send_s, "seam"), send(send_a, "z"), send(both2, "c")
        w = [send(got1, f"x{step}") for step in (1, 2, 3)]
        *w, got_a, got_c, got_s = lax.optimization_barrier((*w, got_a, got_c, got_s))
        send_b, send_f, both3 = call(
            functools.partial(third_kernel, starts[4]),
            (vmem(kb, BLK, BLK), vmem(kf, BLK, BLK), vmem(4 * k1, BLK, BLK)), 1, 9,
        )(table, own, *x, got1, *w, got_c)
        got_b, got_f, got_d = send(send_b, "z"), send(send_f, "far"), send(both3, "c")
        first = [own, *x, got1, *w, got_c, got_s, got_a]
        pool = call(functools.partial(early_kernel, starts[6]), vmem(DUMMY, BLK, BLK), 1, len(first))(table, *first)
        late = starts[6] + sum(q.shape[0] for q in first)
        purified, _ = pl.pallas_call(
            functools.partial(final_kernel, late),
            out_shape=(vmem(1, BLK, KEPT * BLK, dtype=jnp.float32), vmem(DUMMY, BLK, BLK)),
            in_specs=[scalars()] * 2 + [whole()] * 5,
            out_specs=(whole(), whole()),
            scratch_shapes=[pltpu.VMEM((BLK, KEPT * BLK), jnp.float32), pltpu.VMEM((BLK, KEPT * BLK), jnp.bfloat16)],
            input_output_aliases={6: 1},
            compiler_params=pltpu.CompilerParams(vmem_limit_bytes=24 << 20),
        )(table, keep, masked, got_d, got_b, got_f, pool)
        return purified

    return jax.shard_map(
        body,
        mesh=fine,
        in_specs=(P(AXES, None, None), P(AXES, None), P(AXES, None)),
        out_specs=P(AXES, None, None),
        check_vma=False,
    )
```

```python
import functools

import jax
import jax.numpy as jnp
import numpy as np
from jax import lax
from jax.experimental import pallas as pl
from jax.experimental.pallas import tpu as pltpu
from jax.sharding import Mesh, PartitionSpec as P

BLK = 128
BAND_HALF = 8
KEEP_HALF = 10
KEPT = 21
AXES = ("y", "zl", "c", "zh", "x")
UPPER = BAND_HALF + 1
DUMMY = KEPT * UPPER


def canonical(row, offset, n):
    return (row % n, offset) if offset >= 0 else ((row + offset) % n, -offset)


def own_lists(p):
    return list(range(0, 4 - p)) + list(range(8 - p, 9)), list(range(-p - 4, -p)) + list(range(4 - p, 8 - p))


def make_plan(ny, nzl):
    n = ny * nzl * 16

    def place(y, zl, c, zh, x):
        return (((y % ny) * nzl + zl) * 2 + c) * 8 + zh * 4 + x % 4

    coords = [(y, zl, c, zh, x) for y in range(ny) for zl in range(nzl) for c in range(2) for zh in range(2) for x in range(4)]

    def ring(y, zl, zh, step):
        z = zh * nzl + zl
        y += 1 if (step == 1 and zl == nzl - 1) else -1 if (step == -1 and zl == 0) else 0
        z = (z + step) % (2 * nzl)
        return y, z % nzl, z // nzl

    def pad(blocks, k):
        return list(blocks) + [None] * (k - len(blocks))

    need = [{((i - KEEP_HALF + u) % n, o): u * UPPER + o for u in range(KEPT) for o in range(UPPER) if u + o < KEPT} for i in range(n)]
    lists = [own_lists(x) for y, zl, c, zh, x in coords]
    own = [[canonical(i, o, n) for o in range(-8, 9)] for i in range(n)]
    sent1 = [[canonical(i, o, n) for o in same] for i, (same, _) in enumerate(lists)]
    sent2 = [[canonical(i, o, n) for o in same + mixed] for i, (same, mixed) in enumerate(lists)]
    moves = {}
    moves["zh"] = [(i, place(y, zl, c, 1 - zh, x)) for i, (y, zl, c, zh, x) in enumerate(coords)]
    moves["c"] = [(i, place(y, zl, 1 - c, zh, x)) for i, (y, zl, c, zh, x) in enumerate(coords)]
    moves["seam"], moves["z"], moves["far"] = [], [], []
    for i, (y, zl, c, zh, x) in enumerate(coords):
        if (zl, c, zh) in ((0, 0, 0), (nzl - 1, 1, 1)):
            moves["seam"].append((i, place(y, zl, c, 1 - zh, x)))
        y2, zl2, zh2 = ring(y, zl, zh, 1 if c else -1)
        moves["z"].append((i, place(y2, zl2, 1 - c, zh2, x)))
        for step in (1, -1):
            y2, zl2, zh2 = ring(y, zl, zh, step)
            if (zh2 == 0 and x < 2 and step == 1) or (zh2 == 1 and x >= 2 and step == -1):
                moves["far"].append((i, place(y2, zl2, c, zh2, x)))

    def moved(sends, name):
        got = [[None] * len(sends[0]) for _ in range(n)]
        for s, d in moves[name]:
            got[d] = sends[s]
        return got

    def join(*parts):
        return [sum(row, []) for row in zip(*parts)]

    got1 = moved(sent1, "zh")
    got2 = [[sum([sent2[i - i % 4 + q] for q in range(4)], []) for i in range(n)]]
    got3 = [[sum([got1[i - i % 4 + q] for q in range(4)], []) for i in range(n)]]
    stock2 = join(own, *got2)
    stock3 = join(stock2, *got3)
    got_c = moved(join(*got2), "c")
    got_d = moved(join(*got3), "c")
    stock4 = join(stock3, got_c)
    known = [set(row) for row in join(stock4, got_d)]

    def choose(name, stock):
        sends = [[] for _ in range(n)]
        for s, d in moves[name]:
            sends[s] = [b for b in need[d] if b not in known[d] and b in set(stock[s])]
        k = max(map(len, sends))
        sends = [pad(q, k) for q in sends]
        got = moved(sends, name)
        for d in range(n):
            known[d] |= set(got[d])
        return sends, got

    sent_s, got_s = choose("seam", stock2)
    sent_a, got_a = choose("z", stock2)
    sent_b, got_b = choose("z", stock4)
    sent_f, got_f = choose("far", stock4)
    assert all(set(need[d]) <= known[d] for d in range(n))

    def where(sends, stock):
        return np.array([[src.index(b) if b is not None else 0 for b in q] for q, src in zip(sends, stock)], np.int32)

    arrived = join(stock4, got_s, got_a, got_d, got_b, got_f)
    spots = np.full((n, len(arrived[0])), DUMMY, np.int32)
    for i in range(n):
        seen = set()
        for k, b in enumerate(arrived[i]):
            if b in need[i] and b not in seen:
                seen.add(b)
                spots[i, k] = need[i][b]
    parts = [where(sent1, own), where(sent2, own), where(sent_s, stock2), where(sent_a, stock2), where(sent_b, stock4), where(sent_f, stock4), spots]
    starts = np.cumsum([0] + [q.shape[1] for q in parts])
    return moves, np.concatenate(parts, axis=1), [q.shape[1] for q in parts], [int(q) for q in starts]


def vmem(*shape, dtype=jnp.bfloat16):
    return jax.ShapeDtypeStruct(shape, dtype)


def whole():
    return pl.BlockSpec(memory_space=pltpu.VMEM)


def scalars():
    return pl.BlockSpec(memory_space=pltpu.SMEM)


def call(kernel, outs, n_scalar, n_vector, scratch=(), mib=8):
    return pl.pallas_call(
        kernel,
        out_shape=outs,
        in_specs=[scalars()] * n_scalar + [whole()] * n_vector,
        out_specs=jax.tree.map(lambda _: whole(), outs),
        scratch_shapes=scratch,
        compiler_params=pltpu.CompilerParams(vmem_limit_bytes=mib << 20),
    )


def first_kernel(start, table, pattern, strip, masked, own, send1, send2):
    for slot in range(2 * BAND_HALF + 1):
        cols = slice(slot * BLK, (slot + 1) * BLK)
        block = strip[0, :, cols] * pattern[0, slot].astype(jnp.bfloat16)
        masked[:, cols] = block
        own[slot] = block if slot >= BAND_HALF else block.T
    gather(start, table, [own], [send1])
    start += send1.shape[0]

    def pack(k, carry):
        block = own[table[start + k]]
        for peer in range(4):
            send2[peer, k] = block
        return carry

    lax.fori_loop(0, send2.shape[1], pack, 0)


def gather(start, table, sources, outs):
    for out in outs:

        def pack(k, carry, out=out, start=start):
            at = table[start + k]
            low = 0
            for source in sources:
                count = source.shape[0]

                @pl.when((at >= low) & (at < low + count))
                def _(source=source, low=low):
                    out[k] = source[at - low]

                low += count
            return carry

        lax.fori_loop(0, out.shape[0], pack, 0)
        start += out.shape[0]


def gather_kernel(n_sources, start, table, *refs):
    gather(start, table, refs[:n_sources], refs[n_sources:])


def product(left, first, pool, v, width):
    last = KEPT - 1 - first
    blank = jnp.zeros((BLK, BLK), jnp.bfloat16)
    total = None
    for upper in (True, False):

        def block(u, col):
            row, offset = (u, col - u) if upper else (col, u - col)
            return pool[row * UPPER + offset] if (0 if upper else 1) <= offset <= BAND_HALF else blank

        low, high = (v - BAND_HALF, v + width - 1) if upper else (v + 1, v + width - 1 + BAND_HALF)
        low, high = max(first, low), min(last, high)
        if low > high:
            continue
        across = [
            jnp.concatenate([block(u, col) for u in range(low, high + 1)], axis=0 if upper else 1)
            for col in range(v, v + width)
        ]
        part = lax.dot_general(
            left[:, (low - first) * BLK : (high - first + 1) * BLK],
            jnp.concatenate(across, axis=1 if upper else 0),
            (((1,), (0 if upper else 1,)), ((), ())),
            preferred_element_type=jnp.float32,
        )
        total = part if total is None else total + part
    return total


def flags(keep, v, width):
    return jnp.concatenate([jnp.full((1, BLK), keep[0, v + j].astype(jnp.float32)) for j in range(width)], axis=1)


def place(low, spots, sources, pool):
    for source in sources:

        def put(k, carry, source=source, low=low):
            at = spots[low + k]

            @pl.when(at < DUMMY)
            def _():
                pool[at] = source[k]

            return carry

        lax.fori_loop(0, source.shape[0], put, 0)
        low += source.shape[0]


def early_kernel(start, spots, *refs):
    place(start, spots, refs[:-1], refs[-1])


def final_kernel(start, spots, keep, masked, *refs):
    *sources, _, out, pool, square, rounded = refs
    place(start, spots, sources, pool)
    groups = [(v, min(2, KEPT - v)) for v in range(0, KEPT, 2)]
    for v, width in groups:
        cols = slice(v * BLK, (v + width) * BLK)
        value = product(masked, KEEP_HALF - BAND_HALF, pool, v, width) * flags(keep, v, width)
        square[:, cols] = value
        rounded[:, cols] = value.astype(jnp.bfloat16)
    for v, width in groups:
        cols = slice(v * BLK, (v + width) * BLK)
        flag = flags(keep, v, width)
        cube = flag * product(rounded, 0, pool, v, width)
        out[0, :, cols] = flag * (3.0 * square[:, cols] - 2.0 * cube)


def solution(mesh):
    ny, nzl = mesh.shape["row"], mesh.shape["col"] // 2
    moves, tables, counts, starts = make_plan(ny, nzl)
    k1, k2, ks, ka, kb, kf, _ = counts
    fine = Mesh(mesh.devices.reshape(ny, nzl, 2, 2, 4), AXES)

    def send(array, name):
        return lax.ppermute(array, AXES, moves[name])

    def spread(copies):
        return lax.all_to_all(copies, "x", 0, 0).reshape(-1, BLK, BLK)

    def body(density, pattern, keep):
        table = lax.dynamic_index_in_dim(jnp.asarray(tables), lax.axis_index(AXES), 0, keepdims=False)
        masked, own, send1, send2 = call(
            functools.partial(first_kernel, starts[0]),
            (vmem(BLK, 17 * BLK), vmem(17, BLK, BLK), vmem(k1, BLK, BLK), vmem(4, k2, BLK, BLK)), 2, 1,
        )(table, pattern, density)
        got1 = send(send1, "zh")
        x = spread(send2)
        send_s, send_a = call(
            functools.partial(gather_kernel, 2, starts[2]), (vmem(ks, BLK, BLK), vmem(ka, BLK, BLK)), 1, 2,
        )(table, own, x)
        got1, send_s, send_a, x = lax.optimization_barrier((got1, send_s, send_a, x))
        got_s, got_a, got_c = send(send_s, "seam"), send(send_a, "z"), send(x, "c")
        w = spread(jnp.broadcast_to(got1, (4, k1, BLK, BLK)))
        w, got_a, got_c, got_s = lax.optimization_barrier((w, got_a, got_c, got_s))
        send_b, send_f = call(
            functools.partial(gather_kernel, 4, starts[4]), (vmem(kb, BLK, BLK), vmem(kf, BLK, BLK)), 1, 4,
        )(table, own, x, w, got_c)
        got_b, got_f, got_d = send(send_b, "z"), send(send_f, "far"), send(w, "c")
        first = [own, x, w, got_c, got_s, got_a]
        pool = call(functools.partial(early_kernel, starts[6]), vmem(DUMMY, BLK, BLK), 1, len(first))(table, *first)
        late = starts[6] + sum(q.shape[0] for q in first)
        purified, _ = pl.pallas_call(
            functools.partial(final_kernel, late),
            out_shape=(vmem(1, BLK, KEPT * BLK, dtype=jnp.float32), vmem(DUMMY, BLK, BLK)),
            in_specs=[scalars()] * 2 + [whole()] * 5,
            out_specs=(whole(), whole()),
            scratch_shapes=[pltpu.VMEM((BLK, KEPT * BLK), jnp.float32), pltpu.VMEM((BLK, KEPT * BLK), jnp.bfloat16)],
            input_output_aliases={6: 1},
            compiler_params=pltpu.CompilerParams(vmem_limit_bytes=24 << 20),
        )(table, keep, masked, got_d, got_b, got_f, pool)
        return purified

    return jax.shard_map(
        body,
        mesh=fine,
        in_specs=(P(AXES, None, None), P(AXES, None), P(AXES, None)),
        out_specs=P(AXES, None, None),
        check_vma=False,
    )
```

```python
import functools

import jax
import jax.numpy as jnp
import numpy as np
from jax import lax
from jax.experimental import pallas as pl
from jax.experimental.pallas import tpu as pltpu
from jax.sharding import Mesh, PartitionSpec as P

BLK = 128
BAND_HALF = 8
KEEP_HALF = 10
KEPT = 21
AXES = ("y", "zl", "c", "zh", "x")
UPPER = BAND_HALF + 1
DUMMY = KEPT * UPPER


def canonical(row, offset, n):
    return (row % n, offset) if offset >= 0 else ((row + offset) % n, -offset)


def own_lists(p):
    return list(range(0, 4 - p)) + list(range(8 - p, 9)), list(range(-p - 4, -p)) + list(range(4 - p, 8 - p))


def make_plan(ny, nzl):
    n = ny * nzl * 16

    def place(y, zl, c, zh, x):
        return (((y % ny) * nzl + zl) * 2 + c) * 8 + zh * 4 + x % 4

    coords = [(y, zl, c, zh, x) for y in range(ny) for zl in range(nzl) for c in range(2) for zh in range(2) for x in range(4)]

    def ring(y, zl, zh, step):
        z = zh * nzl + zl
        y += 1 if (step == 1 and zl == nzl - 1) else -1 if (step == -1 and zl == 0) else 0
        z = (z + step) % (2 * nzl)
        return y, z % nzl, z // nzl

    def pad(blocks, k):
        return list(blocks) + [None] * (k - len(blocks))

    need = [{((i - KEEP_HALF + u) % n, o): u * UPPER + o for u in range(KEPT) for o in range(UPPER) if u + o < KEPT} for i in range(n)]
    lists = [own_lists(x) for y, zl, c, zh, x in coords]
    own = [[canonical(i, o, n) for o in range(-8, 9)] for i in range(n)]
    sent1 = [[canonical(i, o, n) for o in same] for i, (same, _) in enumerate(lists)]
    sent2 = [[canonical(i, o, n) for o in same + mixed] for i, (same, mixed) in enumerate(lists)]
    moves = {}
    moves["zh"] = [(i, place(y, zl, c, 1 - zh, x)) for i, (y, zl, c, zh, x) in enumerate(coords)]
    moves["c"] = [(i, place(y, zl, 1 - c, zh, x)) for i, (y, zl, c, zh, x) in enumerate(coords)]
    moves["seam"], moves["z"], moves["far"] = [], [], []
    for i, (y, zl, c, zh, x) in enumerate(coords):
        if (zl, c, zh) in ((0, 0, 0), (nzl - 1, 1, 1)):
            moves["seam"].append((i, place(y, zl, c, 1 - zh, x)))
        if (zl, c, zh) == (nzl - 1, 0, 1):
            moves["seam"].append((i, place(y + 1, 0, 0, 0, x)))
        y2, zl2, zh2 = ring(y, zl, zh, 1 if c else -1)
        moves["z"].append((i, place(y2, zl2, 1 - c, zh2, x)))
        for step in (1, -1):
            y2, zl2, zh2 = ring(y, zl, zh, step)
            if (zh2 == 0 and x < 2 and step == 1) or (zh2 == 1 and x >= 2 and step == -1):
                moves["far"].append((i, place(y2, zl2, c, zh2, x)))

    def moved(sends, name):
        got = [[None] * len(sends[0]) for _ in range(n)]
        for s, d in moves[name]:
            got[d] = sends[s]
        return got

    def join(*parts):
        return [sum(row, []) for row in zip(*parts)]

    got1 = moved(sent1, "zh")
    got2 = [[sum([sent2[i - i % 4 + q] for q in range(4)], []) for i in range(n)]]
    got3 = [[sum([got1[i - i % 4 + q] for q in range(4)], []) for i in range(n)]]
    stock2 = join(own, *got2)
    stock3 = join(stock2, *got3)
    got_c = moved(join(*got2), "c")
    got_d = moved(join(*got3), "c")
    stock4 = join(stock3, got_c)
    known = [set(row) for row in join(stock4, got_d)]

    def choose(name, stock):
        sends = [[] for _ in range(n)]
        for s, d in moves[name]:
            sends[s] = [b for b in need[d] if b not in known[d] and b in set(stock[s])]
        k = max(map(len, sends))
        sends = [pad(q, k) for q in sends]
        got = moved(sends, name)
        for d in range(n):
            known[d] |= set(got[d])
        return sends, got

    sent_s, got_s = choose("seam", stock2)
    sent_a, got_a = choose("z", stock2)
    sent_b, got_b = choose("z", stock4)
    sent_f, got_f = choose("far", stock4)
    assert all(set(need[d]) <= known[d] for d in range(n))

    def where(sends, stock):
        return np.array([[src.index(b) if b is not None else 0 for b in q] for q, src in zip(sends, stock)], np.int32)

    arrived = join(stock4, got_s, got_a, got_d, got_b, got_f)
    spots = np.full((n, len(arrived[0])), DUMMY, np.int32)
    for i in range(n):
        seen = set()
        for k, b in enumerate(arrived[i]):
            if b in need[i] and b not in seen:
                seen.add(b)
                spots[i, k] = need[i][b]
    parts = [where(sent_s, stock2), where(sent_a, stock2), where(sent_b, stock4), where(sent_f, stock4), spots]
    starts = np.cumsum([0] + [q.shape[1] for q in parts])
    sizes = [len(lists[0][0]), len(sent2[0])] + [q.shape[1] for q in parts]
    return moves, np.concatenate(parts, axis=1), sizes, [int(q) for q in starts]


def vmem(*shape, dtype=jnp.bfloat16):
    return jax.ShapeDtypeStruct(shape, dtype)


def whole():
    return pl.BlockSpec(memory_space=pltpu.VMEM)


def scalars():
    return pl.BlockSpec(memory_space=pltpu.SMEM)


def call(kernel, outs, n_scalar, n_vector, scratch=(), mib=8):
    return pl.pallas_call(
        kernel,
        out_shape=outs,
        in_specs=[scalars()] * n_scalar + [whole()] * n_vector,
        out_specs=jax.tree.map(lambda _: whole(), outs),
        scratch_shapes=scratch,
        compiler_params=pltpu.CompilerParams(vmem_limit_bytes=mib << 20),
    )


def first_kernel(pattern, strip, masked, own, send1, send2):
    for slot in range(2 * BAND_HALF + 1):
        cols = slice(slot * BLK, (slot + 1) * BLK)
        block = strip[0, :, cols] * pattern[0, slot].astype(jnp.bfloat16)
        masked[:, cols] = block
        own[slot] = block if slot >= BAND_HALF else block.T
    p = lax.axis_index("x")
    for k in range(send2.shape[1]):
        if k < 5:
            offset = jnp.where(k < 4 - p, k, k + 4)
            send1[k] = own[BAND_HALF + offset]
        else:
            offset = k - 9 - p if k < 9 else k - 5 - p
        block = own[BAND_HALF + offset]
        for peer in range(4):
            send2[peer, k] = block


def gather(start, table, sources, outs):
    for out in outs:

        def pack(k, carry, out=out, start=start):
            at = table[start + k]
            low = 0
            for source in sources:
                count = source.shape[0]

                @pl.when((at >= low) & (at < low + count))
                def _(source=source, low=low):
                    out[k] = source[at - low]

                low += count
            return carry

        lax.fori_loop(0, out.shape[0], pack, 0)
        start += out.shape[0]


def gather_kernel(n_sources, start, table, *refs):
    gather(start, table, refs[:n_sources], refs[n_sources:])


def product(left, first, pool, v, width):
    last = KEPT - 1 - first
    blank = jnp.zeros((BLK, BLK), jnp.bfloat16)
    total = None
    for upper in (True, False):

        def block(u, col):
            row, offset = (u, col - u) if upper else (col, u - col)
            return pool[row * UPPER + offset] if (0 if upper else 1) <= offset <= BAND_HALF else blank

        low, high = (v - BAND_HALF, v + width - 1) if upper else (v + 1, v + width - 1 + BAND_HALF)
        low, high = max(first, low), min(last, high)
        if low > high:
            continue
        across = [
            jnp.concatenate([block(u, col) for u in range(low, high + 1)], axis=0 if upper else 1)
            for col in range(v, v + width)
        ]
        part = lax.dot_general(
            left[:, (low - first) * BLK : (high - first + 1) * BLK],
            jnp.concatenate(across, axis=1 if upper else 0),
            (((1,), (0 if upper else 1,)), ((), ())),
            preferred_element_type=jnp.float32,
        )
        total = part if total is None else total + part
    return total


def flags(keep, v, width):
    return jnp.concatenate([jnp.full((1, BLK), keep[0, v + j].astype(jnp.float32)) for j in range(width)], axis=1)


def place(low, spots, sources, pool):
    for source in sources:

        def put(k, carry, source=source, low=low):
            at = spots[low + k]

            @pl.when(at < DUMMY)
            def _():
                pool[at] = source[k]

            return carry

        lax.fori_loop(0, source.shape[0], put, 0)
        low += source.shape[0]


def early_kernel(start, spots, *refs):
    place(start, spots, refs[:-1], refs[-1])


def final_kernel(start, spots, keep, masked, *refs):
    *sources, _, out, pool, square, rounded = refs
    place(start, spots, sources, pool)
    groups = [(v, min(2, KEPT - v)) for v in range(0, KEPT, 2)]
    for v, width in groups:
        cols = slice(v * BLK, (v + width) * BLK)
        value = product(masked, KEEP_HALF - BAND_HALF, pool, v, width) * flags(keep, v, width)
        square[:, cols] = value
        rounded[:, cols] = value.astype(jnp.bfloat16)
    for v, width in groups:
        cols = slice(v * BLK, (v + width) * BLK)
        flag = flags(keep, v, width)
        cube = flag * product(rounded, 0, pool, v, width)
        out[0, :, cols] = flag * (3.0 * square[:, cols] - 2.0 * cube)


def solution(mesh):
    ny, nzl = mesh.shape["row"], mesh.shape["col"] // 2
    moves, tables, counts, starts = make_plan(ny, nzl)
    k1, k2, ks, ka, kb, kf, _ = counts
    fine = Mesh(mesh.devices.reshape(ny, nzl, 2, 2, 4), AXES)

    def send(array, name):
        return lax.ppermute(array, AXES, moves[name])

    def spread(copies):
        return lax.all_to_all(copies, "x", 0, 0).reshape(-1, BLK, BLK)

    def body(density, pattern, keep):
        table = lax.dynamic_index_in_dim(jnp.asarray(tables), lax.axis_index(AXES), 0, keepdims=False)
        masked, own, send1, send2 = call(
            first_kernel,
            (vmem(BLK, 17 * BLK), vmem(17, BLK, BLK), vmem(k1, BLK, BLK), vmem(4, k2, BLK, BLK)), 1, 1,
        )(pattern, density)
        got1 = send(send1, "zh")
        x = spread(send2)
        send_s, send_a = call(
            functools.partial(gather_kernel, 2, starts[0]), (vmem(ks, BLK, BLK), vmem(ka, BLK, BLK)), 1, 2,
        )(table, own, x)
        got1, send_s, send_a, x = lax.optimization_barrier((got1, send_s, send_a, x))
        got_s, got_a, got_c = send(send_s, "seam"), send(send_a, "z"), send(x, "c")
        w = spread(jnp.broadcast_to(got1, (4, k1, BLK, BLK)))
        w, got_c, got_s = lax.optimization_barrier((w, got_c, got_s))
        send_b, send_f = call(
            functools.partial(gather_kernel, 4, starts[2]), (vmem(kb, BLK, BLK), vmem(kf, BLK, BLK)), 1, 4,
        )(table, own, x, w, got_c)
        got_b, got_f, got_d = send(send_b, "z"), send(send_f, "far"), send(w, "c")
        first = [own, x, w, got_c, got_s, got_a]
        pool = call(functools.partial(early_kernel, starts[4]), vmem(DUMMY, BLK, BLK), 1, len(first))(table, *first)
        late = starts[4] + sum(q.shape[0] for q in first)
        purified, _ = pl.pallas_call(
            functools.partial(final_kernel, late),
            out_shape=(vmem(1, BLK, KEPT * BLK, dtype=jnp.float32), vmem(DUMMY, BLK, BLK)),
            in_specs=[scalars()] * 2 + [whole()] * 5,
            out_specs=(whole(), whole()),
            scratch_shapes=[pltpu.VMEM((BLK, KEPT * BLK), jnp.float32), pltpu.VMEM((BLK, KEPT * BLK), jnp.bfloat16)],
            input_output_aliases={6: 1},
            compiler_params=pltpu.CompilerParams(vmem_limit_bytes=24 << 20),
        )(table, keep, masked, got_d, got_b, got_f, pool)
        return purified

    return jax.shard_map(
        body,
        mesh=fine,
        in_specs=(P(AXES, None, None), P(AXES, None), P(AXES, None)),
        out_specs=P(AXES, None, None),
        check_vma=False,
    )
```

```python
import functools

import jax
import jax.numpy as jnp
import numpy as np
from jax import lax
from jax.experimental import pallas as pl
from jax.experimental.pallas import tpu as pltpu
from jax.sharding import Mesh, PartitionSpec as P

BLK = 128
BAND_HALF = 8
KEEP_HALF = 10
KEPT = 21
AXES = ("y", "zl", "c", "zh", "x")
UPPER = BAND_HALF + 1
DUMMY = KEPT * UPPER


def canonical(row, offset, n):
    return (row % n, offset) if offset >= 0 else ((row + offset) % n, -offset)


def own_lists(p):
    return list(range(0, 4 - p)) + list(range(8 - p, 9)), list(range(-p - 4, -p)) + list(range(4 - p, 8 - p))


def make_plan(ny, nzl):
    n = ny * nzl * 16

    def place(y, zl, c, zh, x):
        return (((y % ny) * nzl + zl) * 2 + c) * 8 + zh * 4 + x % 4

    coords = [(y, zl, c, zh, x) for y in range(ny) for zl in range(nzl) for c in range(2) for zh in range(2) for x in range(4)]

    def ring(y, zl, zh, step):
        z = zh * nzl + zl
        y += 1 if (step == 1 and zl == nzl - 1) else -1 if (step == -1 and zl == 0) else 0
        z = (z + step) % (2 * nzl)
        return y, z % nzl, z // nzl

    def pad(blocks, k):
        return list(blocks) + [None] * (k - len(blocks))

    need = [{((i - KEEP_HALF + u) % n, o): u * UPPER + o for u in range(KEPT) for o in range(UPPER) if u + o < KEPT} for i in range(n)]
    lists = [own_lists(x) for y, zl, c, zh, x in coords]
    own = [[canonical(i, o, n) for o in range(-8, 9)] for i in range(n)]
    sent1 = [[canonical(i, o, n) for o in same] for i, (same, _) in enumerate(lists)]
    sent2 = [[canonical(i, o, n) for o in same + mixed] for i, (same, mixed) in enumerate(lists)]
    moves = {}
    moves["zh"] = [(i, place(y, zl, c, 1 - zh, x)) for i, (y, zl, c, zh, x) in enumerate(coords)]
    moves["c"] = [(i, place(y, zl, 1 - c, zh, x)) for i, (y, zl, c, zh, x) in enumerate(coords)]
    moves["seam"], moves["z"], moves["far"] = [], [], []
    for i, (y, zl, c, zh, x) in enumerate(coords):
        if (zl, c, zh) in ((0, 0, 0), (nzl - 1, 1, 1)):
            moves["seam"].append((i, place(y, zl, c, 1 - zh, x)))
        if (zl, c, zh) == (nzl - 1, 0, 1):
            moves["seam"].append((i, place(y + 1, 0, 0, 0, x)))
        y2, zl2, zh2 = ring(y, zl, zh, 1 if c else -1)
        moves["z"].append((i, place(y2, zl2, 1 - c, zh2, x)))
        for step in (1, -1):
            y2, zl2, zh2 = ring(y, zl, zh, step)
            if (zh2 == 0 and x < 2 and step == 1) or (zh2 == 1 and x >= 2 and step == -1):
                moves["far"].append((i, place(y2, zl2, c, zh2, x)))

    def moved(sends, name):
        got = [[None] * len(sends[0]) for _ in range(n)]
        for s, d in moves[name]:
            got[d] = sends[s]
        return got

    def join(*parts):
        return [sum(row, []) for row in zip(*parts)]

    got1 = moved(sent1, "zh")
    got2 = [[sum([sent2[i - i % 4 + q] for q in range(4)], []) for i in range(n)]]
    got3 = [[sum([got1[i - i % 4 + q] for q in range(4)], []) for i in range(n)]]
    stock2 = join(own, *got2)
    stock3 = join(stock2, *got3)
    got_c = moved(join(*got2), "c")
    got_d = moved(join(*got3), "c")
    stock4 = join(stock3, got_c)
    known = [set(row) for row in join(stock4, got_d)]

    def choose(name, stock):
        sends = [[] for _ in range(n)]
        for s, d in moves[name]:
            sends[s] = [b for b in need[d] if b not in known[d] and b in set(stock[s])]
        k = max(map(len, sends))
        sends = [pad(q, k) for q in sends]
        got = moved(sends, name)
        for d in range(n):
            known[d] |= set(got[d])
        return sends, got

    sent_s, got_s = choose("seam", stock2)
    sent_a, got_a = choose("z", stock2)
    sent_b, got_b = choose("z", stock4)
    sent_f, got_f = choose("far", stock4)
    assert all(set(need[d]) <= known[d] for d in range(n))

    def where(sends, stock):
        return np.array([[src.index(b) if b is not None else 0 for b in q] for q, src in zip(sends, stock)], np.int32)

    width = max(len(sent_s[0]), len(sent_b[0]) + 1)
    sent_s, got_s = [pad(q, width) for q in sent_s], [pad(q, width) for q in got_s]
    arrived = join(stock4, got_a, got_d, got_b, got_f, got_s)
    spots = np.full((n, len(arrived[0])), DUMMY, np.int32)
    for i in range(n):
        seen = set()
        for k, b in enumerate(arrived[i]):
            if b in need[i] and b not in seen:
                seen.add(b)
                spots[i, k] = need[i][b]
    parts = [where(sent_s, stock2), where(sent_a, stock2), where(sent_b, stock4), where(sent_f, stock4), spots]
    starts = np.cumsum([0] + [q.shape[1] for q in parts])
    sizes = [len(lists[0][0]), len(sent2[0])] + [q.shape[1] for q in parts]
    return moves, np.concatenate(parts, axis=1), sizes, [int(q) for q in starts]


def vmem(*shape, dtype=jnp.bfloat16):
    return jax.ShapeDtypeStruct(shape, dtype)


def whole():
    return pl.BlockSpec(memory_space=pltpu.VMEM)


def scalars():
    return pl.BlockSpec(memory_space=pltpu.SMEM)


def call(kernel, outs, n_scalar, n_vector, scratch=(), mib=8):
    return pl.pallas_call(
        kernel,
        out_shape=outs,
        in_specs=[scalars()] * n_scalar + [whole()] * n_vector,
        out_specs=jax.tree.map(lambda _: whole(), outs),
        scratch_shapes=scratch,
        compiler_params=pltpu.CompilerParams(vmem_limit_bytes=mib << 20),
    )


def first_kernel(pattern, strip, masked, own, send1, send2):
    for slot in range(2 * BAND_HALF + 1):
        cols = slice(slot * BLK, (slot + 1) * BLK)
        block = strip[0, :, cols] * pattern[0, slot].astype(jnp.bfloat16)
        masked[:, cols] = block
        own[slot] = block if slot >= BAND_HALF else block.T
    p = lax.axis_index("x")
    for k in range(send2.shape[1]):
        if k < 5:
            offset = jnp.where(k < 4 - p, k, k + 4)
            send1[k] = own[BAND_HALF + offset]
        else:
            offset = k - 9 - p if k < 9 else k - 5 - p
        block = own[BAND_HALF + offset]
        for peer in range(4):
            send2[peer, k] = block


def gather(start, table, sources, outs):
    for out in outs:

        def pack(k, carry, out=out, start=start):
            at = table[start + k]
            low = 0
            for source in sources:
                count = source.shape[0]

                @pl.when((at >= low) & (at < low + count))
                def _(source=source, low=low):
                    out[k] = source[at - low]

                low += count
            return carry

        lax.fori_loop(0, out.shape[0], pack, 0)
        start += out.shape[0]


def gather_kernel(n_sources, start, table, *refs):
    gather(start, table, refs[:n_sources], refs[n_sources:])


def product(left, first, pool, v, width):
    last = KEPT - 1 - first
    blank = jnp.zeros((BLK, BLK), jnp.bfloat16)
    total = None
    for upper in (True, False):

        def block(u, col):
            row, offset = (u, col - u) if upper else (col, u - col)
            return pool[row * UPPER + offset] if (0 if upper else 1) <= offset <= BAND_HALF else blank

        low, high = (v - BAND_HALF, v + width - 1) if upper else (v + 1, v + width - 1 + BAND_HALF)
        low, high = max(first, low), min(last, high)
        if low > high:
            continue
        across = [
            jnp.concatenate([block(u, col) for u in range(low, high + 1)], axis=0 if upper else 1)
            for col in range(v, v + width)
        ]
        part = lax.dot_general(
            left[:, (low - first) * BLK : (high - first + 1) * BLK],
            jnp.concatenate(across, axis=1 if upper else 0),
            (((1,), (0 if upper else 1,)), ((), ())),
            preferred_element_type=jnp.float32,
        )
        total = part if total is None else total + part
    return total


def flags(keep, v, width):
    return jnp.concatenate([jnp.full((1, BLK), keep[0, v + j].astype(jnp.float32)) for j in range(width)], axis=1)


def place(low, spots, sources, pool):
    for source in sources:

        def put(k, carry, source=source, low=low):
            at = spots[low + k]

            @pl.when(at < DUMMY)
            def _():
                pool[at] = source[k]

            return carry

        lax.fori_loop(0, source.shape[0], put, 0)
        low += source.shape[0]


def early_kernel(start, spots, *refs):
    place(start, spots, refs[:-1], refs[-1])


def final_kernel(start, spots, keep, masked, *refs):
    *sources, _, out, pool, square, rounded = refs
    place(start, spots, sources, pool)
    groups = [(v, min(2, KEPT - v)) for v in range(0, KEPT, 2)]
    for v, width in groups:
        cols = slice(v * BLK, (v + width) * BLK)
        value = product(masked, KEEP_HALF - BAND_HALF, pool, v, width) * flags(keep, v, width)
        square[:, cols] = value
        rounded[:, cols] = value.astype(jnp.bfloat16)
    for v, width in groups:
        cols = slice(v * BLK, (v + width) * BLK)
        flag = flags(keep, v, width)
        cube = flag * product(rounded, 0, pool, v, width)
        out[0, :, cols] = flag * (3.0 * square[:, cols] - 2.0 * cube)


def solution(mesh):
    ny, nzl = mesh.shape["row"], mesh.shape["col"] // 2
    moves, tables, counts, starts = make_plan(ny, nzl)
    k1, k2, ks, ka, kb, kf, _ = counts
    fine = Mesh(mesh.devices.reshape(ny, nzl, 2, 2, 4), AXES)

    def send(array, name):
        return lax.ppermute(array, AXES, moves[name])

    def spread(copies):
        return lax.all_to_all(copies, "x", 0, 0).reshape(-1, BLK, BLK)

    def body(density, pattern, keep):
        table = lax.dynamic_index_in_dim(jnp.asarray(tables), lax.axis_index(AXES), 0, keepdims=False)
        masked, own, send1, send2 = call(
            first_kernel,
            (vmem(BLK, 17 * BLK), vmem(17, BLK, BLK), vmem(k1, BLK, BLK), vmem(4, k2, BLK, BLK)), 1, 1,
        )(pattern, density)
        got1 = send(send1, "zh")
        x = spread(send2)
        send_s, send_a = call(
            functools.partial(gather_kernel, 2, starts[0]), (vmem(ks, BLK, BLK), vmem(ka, BLK, BLK)), 1, 2,
        )(table, own, x)
        got1, send_s, send_a, x = lax.optimization_barrier((got1, send_s, send_a, x))
        got_a, got_c = send(send_a, "z"), send(x, "c")
        w = spread(jnp.broadcast_to(got1, (4, k1, BLK, BLK)))
        w, got_c, send_s = lax.optimization_barrier((w, got_c, send_s))
        got_s = send(send_s, "seam")
        send_b, send_f = call(
            functools.partial(gather_kernel, 4, starts[2]), (vmem(kb, BLK, BLK), vmem(kf, BLK, BLK)), 1, 4,
        )(table, own, x, w, got_c)
        got_b, got_f, got_d = send(send_b, "z"), send(send_f, "far"), send(w, "c")
        first = [own, x, w, got_c, got_a]
        pool = call(functools.partial(early_kernel, starts[4]), vmem(DUMMY, BLK, BLK), 1, len(first))(table, *first)
        late = starts[4] + sum(q.shape[0] for q in first)
        purified, _ = pl.pallas_call(
            functools.partial(final_kernel, late),
            out_shape=(vmem(1, BLK, KEPT * BLK, dtype=jnp.float32), vmem(DUMMY, BLK, BLK)),
            in_specs=[scalars()] * 2 + [whole()] * 6,
            out_specs=(whole(), whole()),
            scratch_shapes=[pltpu.VMEM((BLK, KEPT * BLK), jnp.float32), pltpu.VMEM((BLK, KEPT * BLK), jnp.bfloat16)],
            input_output_aliases={7: 1},
            compiler_params=pltpu.CompilerParams(vmem_limit_bytes=24 << 20),
        )(table, keep, masked, got_d, got_b, got_f, got_s, pool)
        return purified

    return jax.shard_map(
        body,
        mesh=fine,
        in_specs=(P(AXES, None, None), P(AXES, None), P(AXES, None)),
        out_specs=P(AXES, None, None),
        check_vma=False,
    )
```

```python
import functools

import jax
import jax.numpy as jnp
import numpy as np
from jax import lax
from jax.experimental import pallas as pl
from jax.experimental.pallas import tpu as pltpu
from jax.sharding import Mesh, PartitionSpec as P

BLK = 128
BAND_HALF = 8
KEEP_HALF = 10
KEPT = 21
AXES = ("y", "zl", "c", "zh", "x")
UPPER = BAND_HALF + 1
DUMMY = KEPT * UPPER


def canonical(row, offset, n):
    return (row % n, offset) if offset >= 0 else ((row + offset) % n, -offset)


def own_lists(p):
    return list(range(0, 4 - p)) + list(range(8 - p, 9)), list(range(-p - 4, -p)) + list(range(4 - p, 8 - p))


def make_plan(ny, nzl):
    n = ny * nzl * 16

    def place(y, zl, c, zh, x):
        return (((y % ny) * nzl + zl) * 2 + c) * 8 + zh * 4 + x % 4

    coords = [(y, zl, c, zh, x) for y in range(ny) for zl in range(nzl) for c in range(2) for zh in range(2) for x in range(4)]

    def ring(y, zl, zh, step):
        z = zh * nzl + zl
        y += 1 if (step == 1 and zl == nzl - 1) else -1 if (step == -1 and zl == 0) else 0
        z = (z + step) % (2 * nzl)
        return y, z % nzl, z // nzl

    def pad(blocks, k):
        return list(blocks) + [None] * (k - len(blocks))

    need = [{((i - KEEP_HALF + u) % n, o): u * UPPER + o for u in range(KEPT) for o in range(UPPER) if u + o < KEPT} for i in range(n)]
    lists = [own_lists(x) for y, zl, c, zh, x in coords]
    own = [[canonical(i, o, n) for o in range(-8, 9)] for i in range(n)]
    sent1 = [[canonical(i, o, n) for o in same] for i, (same, _) in enumerate(lists)]
    sent2 = [[canonical(i, o, n) for o in same + mixed] for i, (same, mixed) in enumerate(lists)]
    moves = {}
    moves["zh"] = [(i, place(y, zl, c, 1 - zh, x)) for i, (y, zl, c, zh, x) in enumerate(coords)]
    moves["c"] = [(i, place(y, zl, 1 - c, zh, x)) for i, (y, zl, c, zh, x) in enumerate(coords)]
    moves["seam"], moves["z"], moves["far"] = [], [], []
    for i, (y, zl, c, zh, x) in enumerate(coords):
        if (zl, c, zh) in ((0, 0, 0), (nzl - 1, 1, 1)):
            moves["seam"].append((i, place(y, zl, c, 1 - zh, x)))
        if (zl, c, zh) == (nzl - 1, 0, 1):
            moves["seam"].append((i, place(y + 1, 0, 0, 0, x)))
        y2, zl2, zh2 = ring(y, zl, zh, 1 if c else -1)
        moves["z"].append((i, place(y2, zl2, 1 - c, zh2, x)))
        for step in (1, -1):
            y2, zl2, zh2 = ring(y, zl, zh, step)
            if (zh2 == 0 and x < 2 and step == 1) or (zh2 == 1 and x >= 2 and step == -1):
                moves["far"].append((i, place(y2, zl2, c, zh2, x)))

    def moved(sends, name):
        got = [[None] * len(sends[0]) for _ in range(n)]
        for s, d in moves[name]:
            got[d] = sends[s]
        return got

    def join(*parts):
        return [sum(row, []) for row in zip(*parts)]

    got1 = moved(sent1, "zh")
    got2 = [[sum([sent2[i - i % 4 + q] for q in range(4)], []) for i in range(n)]]
    got3 = [[sum([got1[i - i % 4 + q] for q in range(4)], []) for i in range(n)]]
    stock2 = join(own, *got2)
    stock3 = join(stock2, *got3)
    got_c = moved(join(*got2), "c")
    got_d = moved(join(*got3), "c")
    stock4 = join(stock3, got_c)
    known = [set(row) for row in join(stock4, got_d)]

    def choose(name, stock):
        sends = [[] for _ in range(n)]
        for s, d in moves[name]:
            sends[s] = [b for b in need[d] if b not in known[d] and b in set(stock[s])]
        k = max(map(len, sends))
        sends = [pad(q, k) for q in sends]
        got = moved(sends, name)
        for d in range(n):
            known[d] |= set(got[d])
        return sends, got

    sent_s, got_s = choose("seam", stock2)
    sent_a, got_a = choose("z", stock2)
    sent_b, got_b = choose("z", stock4)
    sent_f, got_f = choose("far", stock4)
    assert all(set(need[d]) <= known[d] for d in range(n))

    def where(sends, stock):
        return np.array([[src.index(b) if b is not None else 0 for b in q] for q, src in zip(sends, stock)], np.int32)

    sent_s, got_s = [pad(q, 24) for q in sent_s], [pad(q, 24) for q in got_s]
    arrived = join(stock4, got_s, got_a, got_d, got_b, got_f)
    spots = np.full((n, len(arrived[0])), DUMMY, np.int32)
    for i in range(n):
        seen = set()
        for k, b in enumerate(arrived[i]):
            if b in need[i] and b not in seen:
                seen.add(b)
                spots[i, k] = need[i][b]
    parts = [where(sent_s, stock2), where(sent_a, stock2), where(sent_b, stock4), where(sent_f, stock4), spots]
    starts = np.cumsum([0] + [q.shape[1] for q in parts])
    sizes = [len(lists[0][0]), len(sent2[0])] + [q.shape[1] for q in parts]
    return moves, np.concatenate(parts, axis=1), sizes, [int(q) for q in starts]


def vmem(*shape, dtype=jnp.bfloat16):
    return jax.ShapeDtypeStruct(shape, dtype)


def whole():
    return pl.BlockSpec(memory_space=pltpu.VMEM)


def scalars():
    return pl.BlockSpec(memory_space=pltpu.SMEM)


def call(kernel, outs, n_scalar, n_vector, scratch=(), mib=8):
    return pl.pallas_call(
        kernel,
        out_shape=outs,
        in_specs=[scalars()] * n_scalar + [whole()] * n_vector,
        out_specs=jax.tree.map(lambda _: whole(), outs),
        scratch_shapes=scratch,
        compiler_params=pltpu.CompilerParams(vmem_limit_bytes=mib << 20),
    )


def first_kernel(pattern, strip, masked, own, send1, send2):
    for slot in range(2 * BAND_HALF + 1):
        cols = slice(slot * BLK, (slot + 1) * BLK)
        block = strip[0, :, cols] * pattern[0, slot].astype(jnp.bfloat16)
        masked[:, cols] = block
        own[slot] = block if slot >= BAND_HALF else block.T
    p = lax.axis_index("x")
    for k in range(send2.shape[1]):
        if k < 5:
            offset = jnp.where(k < 4 - p, k, k + 4)
            send1[k] = own[BAND_HALF + offset]
        else:
            offset = k - 9 - p if k < 9 else k - 5 - p
        block = own[BAND_HALF + offset]
        for peer in range(4):
            send2[peer, k] = block


def gather(start, table, sources, outs):
    for out in outs:

        def pack(k, carry, out=out, start=start):
            at = table[start + k]
            low = 0
            for source in sources:
                count = source.shape[0]

                @pl.when((at >= low) & (at < low + count))
                def _(source=source, low=low):
                    out[k] = source[at - low]

                low += count
            return carry

        lax.fori_loop(0, out.shape[0], pack, 0)
        start += out.shape[0]


def gather_kernel(n_sources, start, table, *refs):
    gather(start, table, refs[:n_sources], refs[n_sources:])


def product(left, first, pool, v, width):
    last = KEPT - 1 - first
    blank = jnp.zeros((BLK, BLK), jnp.bfloat16)
    total = None
    for upper in (True, False):

        def block(u, col):
            row, offset = (u, col - u) if upper else (col, u - col)
            return pool[row * UPPER + offset] if (0 if upper else 1) <= offset <= BAND_HALF else blank

        low, high = (v - BAND_HALF, v + width - 1) if upper else (v + 1, v + width - 1 + BAND_HALF)
        low, high = max(first, low), min(last, high)
        if low > high:
            continue
        across = [
            jnp.concatenate([block(u, col) for u in range(low, high + 1)], axis=0 if upper else 1)
            for col in range(v, v + width)
        ]
        part = lax.dot_general(
            left[:, (low - first) * BLK : (high - first + 1) * BLK],
            jnp.concatenate(across, axis=1 if upper else 0),
            (((1,), (0 if upper else 1,)), ((), ())),
            preferred_element_type=jnp.float32,
        )
        total = part if total is None else total + part
    return total


def flags(keep, v, width):
    return jnp.concatenate([jnp.full((1, BLK), keep[0, v + j].astype(jnp.float32)) for j in range(width)], axis=1)


def place(low, spots, sources, pool):
    for source in sources:

        def put(k, carry, source=source, low=low):
            at = spots[low + k]

            @pl.when(at < DUMMY)
            def _():
                pool[at] = source[k]

            return carry

        lax.fori_loop(0, source.shape[0], put, 0)
        low += source.shape[0]


def early_kernel(start, spots, *refs):
    place(start, spots, refs[:-1], refs[-1])


def final_kernel(start, spots, keep, masked, *refs):
    *sources, _, out, pool, square, rounded = refs
    place(start, spots, sources, pool)
    groups = [(v, min(2, KEPT - v)) for v in range(0, KEPT, 2)]
    for v, width in groups:
        cols = slice(v * BLK, (v + width) * BLK)
        value = product(masked, KEEP_HALF - BAND_HALF, pool, v, width) * flags(keep, v, width)
        square[:, cols] = value
        rounded[:, cols] = value.astype(jnp.bfloat16)
    for v, width in groups:
        cols = slice(v * BLK, (v + width) * BLK)
        flag = flags(keep, v, width)
        cube = flag * product(rounded, 0, pool, v, width)
        out[0, :, cols] = flag * (3.0 * square[:, cols] - 2.0 * cube)


def solution(mesh):
    ny, nzl = mesh.shape["row"], mesh.shape["col"] // 2
    moves, tables, counts, starts = make_plan(ny, nzl)
    k1, k2, ks, ka, kb, kf, _ = counts
    fine = Mesh(mesh.devices.reshape(ny, nzl, 2, 2, 4), AXES)

    def send(array, name):
        return lax.ppermute(array, AXES, moves[name])

    def spread(copies):
        return lax.all_to_all(copies, "x", 0, 0).reshape(-1, BLK, BLK)

    def body(density, pattern, keep):
        table = lax.dynamic_index_in_dim(jnp.asarray(tables), lax.axis_index(AXES), 0, keepdims=False)
        masked, own, send1, send2 = call(
            first_kernel,
            (vmem(BLK, 17 * BLK), vmem(17, BLK, BLK), vmem(k1, BLK, BLK), vmem(4, k2, BLK, BLK)), 1, 1,
        )(pattern, density)
        got1 = send(send1, "zh")
        x = spread(send2)
        send_s = call(functools.partial(gather_kernel, 2, starts[0]), vmem(ks, BLK, BLK), 1, 2)(table, own, x)
        got1, send_s, x = lax.optimization_barrier((got1, send_s, x))
        got_s, got_c = send(send_s, "seam"), send(x, "c")
        own, x, got_c = lax.optimization_barrier((own, x, got_c))
        send_a = call(functools.partial(gather_kernel, 2, starts[1]), vmem(ka, BLK, BLK), 1, 2)(table, own, x)
        got_a = send(send_a, "z")
        w = spread(jnp.broadcast_to(got1, (4, k1, BLK, BLK)))
        w, got_s = lax.optimization_barrier((w, got_s))
        send_b, send_f = call(
            functools.partial(gather_kernel, 4, starts[2]), (vmem(kb, BLK, BLK), vmem(kf, BLK, BLK)), 1, 4,
        )(table, own, x, w, got_c)
        got_b, got_f, got_d = send(send_b, "z"), send(send_f, "far"), send(w, "c")
        first = [own, x, w, got_c, got_s, got_a]
        pool = call(functools.partial(early_kernel, starts[4]), vmem(DUMMY, BLK, BLK), 1, len(first))(table, *first)
        late = starts[4] + sum(q.shape[0] for q in first)
        purified, _ = pl.pallas_call(
            functools.partial(final_kernel, late),
            out_shape=(vmem(1, BLK, KEPT * BLK, dtype=jnp.float32), vmem(DUMMY, BLK, BLK)),
            in_specs=[scalars()] * 2 + [whole()] * 5,
            out_specs=(whole(), whole()),
            scratch_shapes=[pltpu.VMEM((BLK, KEPT * BLK), jnp.float32), pltpu.VMEM((BLK, KEPT * BLK), jnp.bfloat16)],
            input_output_aliases={6: 1},
            compiler_params=pltpu.CompilerParams(vmem_limit_bytes=24 << 20),
        )(table, keep, masked, got_d, got_b, got_f, pool)
        return purified

    return jax.shard_map(
        body,
        mesh=fine,
        in_specs=(P(AXES, None, None), P(AXES, None), P(AXES, None)),
        out_specs=P(AXES, None, None),
        check_vma=False,
    )
```

```python
import functools

import jax
import jax.numpy as jnp
import numpy as np
from jax import lax
from jax.experimental import pallas as pl
from jax.experimental.pallas import tpu as pltpu
from jax.sharding import Mesh, PartitionSpec as P

BLK = 128
BAND_HALF = 8
KEEP_HALF = 10
KEPT = 21
AXES = ("y", "zl", "c", "zh", "x")
UPPER = BAND_HALF + 1
DUMMY = KEPT * UPPER


def canonical(row, offset, n):
    return (row % n, offset) if offset >= 0 else ((row + offset) % n, -offset)


def own_lists(p):
    return list(range(0, 4 - p)) + list(range(8 - p, 9)), list(range(-p - 4, -p)) + list(range(4 - p, 8 - p))


def is_edge(nzl, zl, zh, x):
    return ((zl == nzl - 1) & (zh == 1) & (x >= 2)) | ((zl == 0) & (zh == 0) & (x < 2))


def make_plan(ny, nzl):
    n = ny * nzl * 16

    def place(y, zl, c, zh, x):
        return (((y % ny) * nzl + zl) * 2 + c) * 8 + zh * 4 + x % 4

    coords = [(y, zl, c, zh, x) for y in range(ny) for zl in range(nzl) for c in range(2) for zh in range(2) for x in range(4)]

    def ring(y, zl, zh, step):
        z = zh * nzl + zl
        y += 1 if (step == 1 and zl == nzl - 1) else -1 if (step == -1 and zl == 0) else 0
        z = (z + step) % (2 * nzl)
        return y, z % nzl, z // nzl

    def pad(blocks, k):
        return list(blocks) + [None] * (k - len(blocks))

    need = [{((i - KEEP_HALF + u) % n, o): u * UPPER + o for u in range(KEPT) for o in range(UPPER) if u + o < KEPT} for i in range(n)]
    lists = [own_lists(x) for y, zl, c, zh, x in coords]
    own = [[canonical(i, o, n) for o in range(-8, 9)] for i in range(n)]
    sent1 = [[canonical(i, o, n) for o in same] for i, (same, _) in enumerate(lists)]
    sent2 = [[canonical(i, o, n) for o in same + mixed] for i, (same, mixed) in enumerate(lists)]
    moves = {}
    moves["zh"] = [(i, place(y, zl, c, 1 - zh, x)) for i, (y, zl, c, zh, x) in enumerate(coords)]
    moves["c"] = [(i, place(y, zl, 1 - c, zh, x)) for i, (y, zl, c, zh, x) in enumerate(coords)]
    moves["seam"], moves["z"], moves["far"], moves["wide"] = [], [], [], []
    for i, (y, zl, c, zh, x) in enumerate(coords):
        if (zl, c, zh) in ((0, 0, 0), (nzl - 1, 1, 1)):
            moves["seam"].append((i, place(y, zl, c, 1 - zh, x)))
        if (zl, c, zh) == (nzl - 1, 0, 1):
            moves["seam"].append((i, place(y + 1, 0, 0, 0, x)))
        y2, zl2, zh2 = ring(y, zl, zh, 1 if c else -1)
        moves["z"].append((i, place(y2, zl2, 1 - c, zh2, x)))
        step = 1 if x >= 2 else -1
        y2, zl2, zh2 = ring(y, zl, zh, step)
        if (zh2 == 0) == (step == 1):
            moves["far"].append((i, place(y2, zl2, c, zh2, x - 2 * step)))
            if x in (0, 3):
                moves["wide"].append((i, place(y2, zl2, c, zh2, 3 - x)))

    def moved(sends, name):
        got = [[None] * len(sends[0]) for _ in range(n)]
        for s, d in moves[name]:
            got[d] = sends[s]
        return got

    def join(*parts):
        return [sum(row, []) for row in zip(*parts)]

    got1 = moved(sent1, "zh")
    got2 = [[sum([sent2[i - i % 4 + q] for q in range(4)], []) for i in range(n)]]
    got3 = [[sum([got1[i - i % 4 + q] for q in range(4)], []) for i in range(n)]]
    stock2 = join(own, *got2)
    stock3 = join(stock2, *got3)
    got_c = moved(join(*got2), "c")
    got_d = moved(join(*got3), "c")
    stock4 = join(stock3, got_c)
    edge = [(sent1 if is_edge(nzl, zl, zh, x) else got1)[i] for i, (y, zl, c, zh, x) in enumerate(coords)]
    got_f, got_w = moved(edge, "far"), moved(edge, "wide")
    known = [set(row) for row in join(stock4, got_d, got_f, got_w)]

    def choose(name, stock):
        sends = [[] for _ in range(n)]
        for s, d in moves[name]:
            sends[s] = [b for b in need[d] if b not in known[d] and b in set(stock[s])]
        k = max(map(len, sends))
        sends = [pad(q, k) for q in sends]
        got = moved(sends, name)
        for d in range(n):
            known[d] |= set(got[d])
        return sends, got

    sent_s, got_s = choose("seam", stock2)
    sent_a, got_a = choose("z", stock2)
    sent_b, got_b = choose("z", stock4)
    assert all(set(need[d]) <= known[d] for d in range(n))

    def where(sends, stock):
        return np.array([[src.index(b) if b is not None else 0 for b in q] for q, src in zip(sends, stock)], np.int32)

    sent_s, got_s = [pad(q, 24) for q in sent_s], [pad(q, 24) for q in got_s]
    arrived = join(stock4, got_s, got_a, got_d, got_b, got_f, got_w)
    spots = np.full((n, len(arrived[0])), DUMMY, np.int32)
    for i in range(n):
        seen = set()
        for k, b in enumerate(arrived[i]):
            if b in need[i] and b not in seen:
                seen.add(b)
                spots[i, k] = need[i][b]
    parts = [where(sent_s, stock2), where(sent_a, stock2), where(sent_b, stock4), spots]
    starts = np.cumsum([0] + [q.shape[1] for q in parts])
    sizes = [len(lists[0][0]), len(sent2[0])] + [q.shape[1] for q in parts]
    return moves, np.concatenate(parts, axis=1), sizes, [int(q) for q in starts]


def vmem(*shape, dtype=jnp.bfloat16):
    return jax.ShapeDtypeStruct(shape, dtype)


def whole():
    return pl.BlockSpec(memory_space=pltpu.VMEM)


def scalars():
    return pl.BlockSpec(memory_space=pltpu.SMEM)


def call(kernel, outs, n_scalar, n_vector, scratch=(), mib=4):
    return pl.pallas_call(
        kernel,
        out_shape=outs,
        in_specs=[scalars()] * n_scalar + [whole()] * n_vector,
        out_specs=jax.tree.map(lambda _: whole(), outs),
        scratch_shapes=scratch,
        compiler_params=pltpu.CompilerParams(vmem_limit_bytes=mib << 20),
    )


def first_kernel(pattern, strip, masked, own, send1, send2):
    for slot in range(2 * BAND_HALF + 1):
        cols = slice(slot * BLK, (slot + 1) * BLK)
        block = strip[0, :, cols] * pattern[0, slot].astype(jnp.bfloat16)
        masked[:, cols] = block
        own[slot] = block if slot >= BAND_HALF else block.T
    p = lax.axis_index("x")
    for k in range(send2.shape[1]):
        if k < 5:
            offset = jnp.where(k < 4 - p, k, k + 4)
            send1[k] = own[BAND_HALF + offset]
        else:
            offset = k - 9 - p if k < 9 else k - 5 - p
        block = own[BAND_HALF + offset]
        for peer in range(4):
            send2[peer, k] = block


def gather(start, table, sources, outs):
    for out in outs:

        def pack(k, carry, out=out, start=start):
            at = table[start + k]
            low = 0
            for source in sources:
                count = source.shape[0]

                @pl.when((at >= low) & (at < low + count))
                def _(source=source, low=low):
                    out[k] = source[at - low]

                low += count
            return carry

        lax.fori_loop(0, out.shape[0], pack, 0)
        start += out.shape[0]


def gather_kernel(n_sources, start, table, *refs):
    gather(start, table, refs[:n_sources], refs[n_sources:])


def product(left, first, pool, v, width):
    last = KEPT - 1 - first
    blank = jnp.zeros((BLK, BLK), jnp.bfloat16)
    total = None
    for upper in (True, False):

        def block(u, col):
            row, offset = (u, col - u) if upper else (col, u - col)
            return pool[row * UPPER + offset] if (0 if upper else 1) <= offset <= BAND_HALF else blank

        low, high = (v - BAND_HALF, v + width - 1) if upper else (v + 1, v + width - 1 + BAND_HALF)
        low, high = max(first, low), min(last, high)
        if low > high:
            continue
        across = [
            jnp.concatenate([block(u, col) for u in range(low, high + 1)], axis=0 if upper else 1)
            for col in range(v, v + width)
        ]
        part = lax.dot_general(
            left[:, (low - first) * BLK : (high - first + 1) * BLK],
            jnp.concatenate(across, axis=1 if upper else 0),
            (((1,), (0 if upper else 1,)), ((), ())),
            preferred_element_type=jnp.float32,
        )
        total = part if total is None else total + part
    return total


def flags(keep, v, width):
    return jnp.concatenate([jnp.full((1, BLK), keep[0, v + j].astype(jnp.float32)) for j in range(width)], axis=1)


def place(low, spots, sources, pool):
    for source in sources:

        def put(k, carry, source=source, low=low):
            at = spots[low + k]

            @pl.when(at < DUMMY)
            def _():
                pool[at] = source[k]

            return carry

        lax.fori_loop(0, source.shape[0], put, 0)
        low += source.shape[0]


def early_kernel(start, spots, *refs):
    place(start, spots, refs[:-1], refs[-1])


def final_kernel(start, spots, keep, masked, *refs):
    *sources, _, out, pool, square, rounded = refs
    place(start, spots, sources, pool)
    groups = [(v, min(2, KEPT - v)) for v in range(0, KEPT, 2)]
    for v, width in groups:
        cols = slice(v * BLK, (v + width) * BLK)
        value = product(masked, KEEP_HALF - BAND_HALF, pool, v, width) * flags(keep, v, width)
        square[:, cols] = value
        rounded[:, cols] = value.astype(jnp.bfloat16)
    for v, width in groups:
        cols = slice(v * BLK, (v + width) * BLK)
        flag = flags(keep, v, width)
        cube = flag * product(rounded, 0, pool, v, width)
        out[0, :, cols] = flag * (3.0 * square[:, cols] - 2.0 * cube)


def solution(mesh):
    ny, nzl = mesh.shape["row"], mesh.shape["col"] // 2
    moves, tables, counts, starts = make_plan(ny, nzl)
    k1, k2, ks, ka, kb, _ = counts
    fine = Mesh(mesh.devices.reshape(ny, nzl, 2, 2, 4), AXES)

    def send(array, name):
        return lax.ppermute(array, AXES, moves[name])

    def spread(copies):
        return lax.all_to_all(copies, "x", 0, 0).reshape(-1, BLK, BLK)

    def body(density, pattern, keep):
        table = lax.dynamic_index_in_dim(jnp.asarray(tables), lax.axis_index(AXES), 0, keepdims=False)
        masked, own, send1, send2 = call(
            first_kernel,
            (vmem(BLK, 17 * BLK), vmem(17, BLK, BLK), vmem(k1, BLK, BLK), vmem(4, k2, BLK, BLK)), 1, 1,
        )(pattern, density)
        got1 = send(send1, "zh")
        x = spread(send2)
        send_s = call(functools.partial(gather_kernel, 2, starts[0]), vmem(ks, BLK, BLK), 1, 2)(table, own, x)
        got1, send_s, x = lax.optimization_barrier((got1, send_s, x))
        got_s, got_c = send(send_s, "seam"), send(x, "c")
        own, x, got_c = lax.optimization_barrier((own, x, got_c))
        send_a = call(functools.partial(gather_kernel, 2, starts[1]), vmem(ka, BLK, BLK), 1, 2)(table, own, x)
        got_a = send(send_a, "z")
        at = lax.axis_index
        edge = jnp.where(is_edge(nzl, at("zl"), at("zh"), at("x")), send1, got1)
        got_f, got_w = send(edge, "far"), send(edge, "wide")
        w = spread(jnp.broadcast_to(got1, (4, k1, BLK, BLK)))
        w, got_s = lax.optimization_barrier((w, got_s))
        send_b = call(functools.partial(gather_kernel, 4, starts[2]), vmem(kb, BLK, BLK), 1, 4)(table, own, x, w, got_c)
        got_b, got_d = send(send_b, "z"), send(w, "c")
        first = [own, x, w, got_c, got_s, got_a]
        pool = call(functools.partial(early_kernel, starts[3]), vmem(DUMMY, BLK, BLK), 1, len(first))(table, *first)
        late = starts[3] + sum(q.shape[0] for q in first)
        purified, _ = pl.pallas_call(
            functools.partial(final_kernel, late),
            out_shape=(vmem(1, BLK, KEPT * BLK, dtype=jnp.float32), vmem(DUMMY, BLK, BLK)),
            in_specs=[scalars()] * 2 + [whole()] * 6,
            out_specs=(whole(), whole()),
            scratch_shapes=[pltpu.VMEM((BLK, KEPT * BLK), jnp.float32), pltpu.VMEM((BLK, KEPT * BLK), jnp.bfloat16)],
            input_output_aliases={7: 1},
            compiler_params=pltpu.CompilerParams(vmem_limit_bytes=10 << 20),
        )(table, keep, masked, got_d, got_b, got_f, got_w, pool)
        return purified

    return jax.shard_map(
        body,
        mesh=fine,
        in_specs=(P(AXES, None, None), P(AXES, None), P(AXES, None)),
        out_specs=P(AXES, None, None),
        check_vma=False,
    )
```

```python
import functools

import jax
import jax.numpy as jnp
import numpy as np
from jax import lax
from jax.experimental import pallas as pl
from jax.experimental.pallas import tpu as pltpu
from jax.sharding import Mesh, PartitionSpec as P

BLK = 128
BAND_HALF = 8
KEEP_HALF = 10
KEPT = 21
AXES = ("y", "zl", "c", "zh", "x")
UPPER = BAND_HALF + 1
DUMMY = KEPT * UPPER


def canonical(row, offset, n):
    return (row % n, offset) if offset >= 0 else ((row + offset) % n, -offset)


def own_lists(p):
    return list(range(0, 4 - p)) + list(range(8 - p, 9)), list(range(-p - 4, -p)) + list(range(4 - p, 8 - p))


def is_edge(nzl, zl, zh, x):
    return ((zl == nzl - 1) & (zh == 1) & (x >= 2)) | ((zl == 0) & (zh == 0) & (x < 2))


def make_plan(ny, nzl):
    n = ny * nzl * 16

    def place(y, zl, c, zh, x):
        return (((y % ny) * nzl + zl) * 2 + c) * 8 + zh * 4 + x % 4

    coords = [(y, zl, c, zh, x) for y in range(ny) for zl in range(nzl) for c in range(2) for zh in range(2) for x in range(4)]

    def ring(y, zl, zh, step):
        z = zh * nzl + zl
        y += 1 if (step == 1 and zl == nzl - 1) else -1 if (step == -1 and zl == 0) else 0
        z = (z + step) % (2 * nzl)
        return y, z % nzl, z // nzl

    def pad(blocks, k):
        return list(blocks) + [None] * (k - len(blocks))

    need = [{((i - KEEP_HALF + u) % n, o): u * UPPER + o for u in range(KEPT) for o in range(UPPER) if u + o < KEPT} for i in range(n)]
    lists = [own_lists(x) for y, zl, c, zh, x in coords]
    own = [[canonical(i, o, n) for o in range(-8, 9)] for i in range(n)]
    sent1 = [[canonical(i, o, n) for o in same] for i, (same, _) in enumerate(lists)]
    sent2 = [[canonical(i, o, n) for o in same + mixed] for i, (same, mixed) in enumerate(lists)]
    moves = {}
    moves["zh"] = [(i, place(y, zl, c, 1 - zh, x)) for i, (y, zl, c, zh, x) in enumerate(coords)]
    moves["c"] = [(i, place(y, zl, 1 - c, zh, x)) for i, (y, zl, c, zh, x) in enumerate(coords)]
    moves["seam"], moves["z"], moves["far"], moves["wide"] = [], [], [], []
    for i, (y, zl, c, zh, x) in enumerate(coords):
        if (zl, c, zh) in ((0, 0, 0), (nzl - 1, 1, 1)):
            moves["seam"].append((i, place(y, zl, c, 1 - zh, x)))
        if (zl, c, zh) == (nzl - 1, 0, 1):
            moves["seam"].append((i, place(y + 1, 0, 0, 0, x)))
        y2, zl2, zh2 = ring(y, zl, zh, 1 if c else -1)
        moves["z"].append((i, place(y2, zl2, 1 - c, zh2, x)))
        step = 1 if x >= 2 else -1
        y2, zl2, zh2 = ring(y, zl, zh, step)
        if (zh2 == 0) == (step == 1):
            moves["far"].append((i, place(y2, zl2, c, zh2, x - 2 * step)))
            if x in (0, 3):
                moves["wide"].append((i, place(y2, zl2, c, zh2, 3 - x)))

    def moved(sends, name):
        got = [[None] * len(sends[0]) for _ in range(n)]
        for s, d in moves[name]:
            got[d] = sends[s]
        return got

    def join(*parts):
        return [sum(row, []) for row in zip(*parts)]

    got1 = moved(sent1, "zh")
    got2 = [[sum([sent2[i - i % 4 + q] for q in range(4)], []) for i in range(n)]]
    got3 = [[sum([got1[i - i % 4 + q] for q in range(4)], []) for i in range(n)]]
    stock2 = join(own, *got2)
    stock3 = join(stock2, *got3)
    got_c = moved(join(*got2), "c")
    got_d = moved(join(*got3), "c")
    stock4 = join(stock3, got_c)
    edge = [(sent1 if is_edge(nzl, zl, zh, x) else got1)[i] for i, (y, zl, c, zh, x) in enumerate(coords)]
    got_f, got_w = moved(edge, "far"), moved(edge, "wide")
    known = [set(row) for row in join(stock4, got_d, got_f, got_w)]

    def choose(name, stock):
        sends = [[] for _ in range(n)]
        for s, d in moves[name]:
            sends[s] = [b for b in need[d] if b not in known[d] and b in set(stock[s])]
        k = max(map(len, sends))
        sends = [pad(q, k) for q in sends]
        got = moved(sends, name)
        for d in range(n):
            known[d] |= set(got[d])
        return sends, got

    sent_s, got_s = choose("seam", stock2)
    sent_a, got_a = choose("z", stock2)
    sent_b, got_b = choose("z", stock4)
    assert all(set(need[d]) <= known[d] for d in range(n))

    def where(sends, stock):
        return np.array([[src.index(b) if b is not None else 0 for b in q] for q, src in zip(sends, stock)], np.int32)

    sent_s, got_s = [pad(q, 24) for q in sent_s], [pad(q, 24) for q in got_s]
    arrived = join(stock4, got_s, got_a, got_d, got_b, got_f, got_w)
    spots = np.full((n, len(arrived[0])), DUMMY, np.int32)
    for i in range(n):
        seen = set()
        for k, b in enumerate(arrived[i]):
            if b in need[i] and b not in seen:
                seen.add(b)
                spots[i, k] = need[i][b]
    parts = [where(sent_s, stock2), where(sent_a, stock2), where(sent_b, stock4), spots]
    starts = np.cumsum([0] + [q.shape[1] for q in parts])
    sizes = [len(lists[0][0]), len(sent2[0])] + [q.shape[1] for q in parts]
    return moves, np.concatenate(parts, axis=1), sizes, [int(q) for q in starts]


def vmem(*shape, dtype=jnp.bfloat16):
    return jax.ShapeDtypeStruct(shape, dtype)


def whole():
    return pl.BlockSpec(memory_space=pltpu.VMEM)


def scalars():
    return pl.BlockSpec(memory_space=pltpu.SMEM)


def call(kernel, outs, n_scalar, n_vector, scratch=(), mib=4):
    return pl.pallas_call(
        kernel,
        out_shape=outs,
        in_specs=[scalars()] * n_scalar + [whole()] * n_vector,
        out_specs=jax.tree.map(lambda _: whole(), outs),
        scratch_shapes=scratch,
        compiler_params=pltpu.CompilerParams(vmem_limit_bytes=mib << 20),
    )


def first_kernel(pattern, strip, masked, own, send1, send2):
    for slot in range(2 * BAND_HALF + 1):
        cols = slice(slot * BLK, (slot + 1) * BLK)
        block = strip[0, :, cols] * pattern[0, slot].astype(jnp.bfloat16)
        masked[:, cols] = block
        own[slot] = block if slot >= BAND_HALF else block.T
    p = lax.axis_index("x")
    for k in range(send2.shape[1]):
        if k < 5:
            offset = jnp.where(k < 4 - p, k, k + 4)
            send1[k] = own[BAND_HALF + offset]
        else:
            offset = k - 9 - p if k < 9 else k - 5 - p
        block = own[BAND_HALF + offset]
        for peer in range(4):
            send2[peer, k] = block


def gather(start, table, sources, outs):
    for out in outs:

        def pack(k, carry, out=out, start=start):
            at = table[start + k]
            low = 0
            for source in sources:
                count = source.shape[0]

                @pl.when((at >= low) & (at < low + count))
                def _(source=source, low=low):
                    out[k] = source[at - low]

                low += count
            return carry

        lax.fori_loop(0, out.shape[0], pack, 0)
        start += out.shape[0]


def gather_kernel(n_sources, start, table, *refs):
    gather(start, table, refs[:n_sources], refs[n_sources:])


def third_kernel(nzl, start, table, own, x, send1, got1, z, edge):
    gather(start, table, [own, x], [z])
    at = lax.axis_index
    swap = is_edge(nzl, at("zl"), at("zh"), at("x"))

    @pl.when(swap)
    def _():
        edge[...] = send1[...]

    @pl.when(jnp.logical_not(swap))
    def _():
        edge[...] = got1[...]


def product(left, first, pool, v, width):
    last = KEPT - 1 - first
    blank = jnp.zeros((BLK, BLK), jnp.bfloat16)
    total = None
    for upper in (True, False):

        def block(u, col):
            row, offset = (u, col - u) if upper else (col, u - col)
            return pool[row * UPPER + offset] if (0 if upper else 1) <= offset <= BAND_HALF else blank

        low, high = (v - BAND_HALF, v + width - 1) if upper else (v + 1, v + width - 1 + BAND_HALF)
        low, high = max(first, low), min(last, high)
        if low > high:
            continue
        across = [
            jnp.concatenate([block(u, col) for u in range(low, high + 1)], axis=0 if upper else 1)
            for col in range(v, v + width)
        ]
        part = lax.dot_general(
            left[:, (low - first) * BLK : (high - first + 1) * BLK],
            jnp.concatenate(across, axis=1 if upper else 0),
            (((1,), (0 if upper else 1,)), ((), ())),
            preferred_element_type=jnp.float32,
        )
        total = part if total is None else total + part
    return total


def flags(keep, v, width):
    return jnp.concatenate([jnp.full((1, BLK), keep[0, v + j].astype(jnp.float32)) for j in range(width)], axis=1)


def place(low, spots, sources, pool):
    for source in sources:

        def put(k, carry, source=source, low=low):
            at = spots[low + k]

            @pl.when(at < DUMMY)
            def _():
                pool[at] = source[k]

            return carry

        lax.fori_loop(0, source.shape[0], put, 0)
        low += source.shape[0]


def early_kernel(start, spots, *refs):
    place(start, spots, refs[:-1], refs[-1])


def final_kernel(start, spots, keep, masked, *refs):
    *sources, _, out, pool, square, rounded = refs
    place(start, spots, sources, pool)
    groups = [(v, min(2, KEPT - v)) for v in range(0, KEPT, 2)]
    for v, width in groups:
        cols = slice(v * BLK, (v + width) * BLK)
        value = product(masked, KEEP_HALF - BAND_HALF, pool, v, width) * flags(keep, v, width)
        square[:, cols] = value
        rounded[:, cols] = value.astype(jnp.bfloat16)
    for v, width in groups:
        cols = slice(v * BLK, (v + width) * BLK)
        flag = flags(keep, v, width)
        cube = flag * product(rounded, 0, pool, v, width)
        out[0, :, cols] = flag * (3.0 * square[:, cols] - 2.0 * cube)


def solution(mesh):
    ny, nzl = mesh.shape["row"], mesh.shape["col"] // 2
    moves, tables, counts, starts = make_plan(ny, nzl)
    k1, k2, ks, ka, kb, _ = counts
    fine = Mesh(mesh.devices.reshape(ny, nzl, 2, 2, 4), AXES)

    def send(array, name):
        return lax.ppermute(array, AXES, moves[name])

    def spread(copies):
        return lax.all_to_all(copies, "x", 0, 0).reshape(-1, BLK, BLK)

    def body(density, pattern, keep):
        table = lax.dynamic_index_in_dim(jnp.asarray(tables), lax.axis_index(AXES), 0, keepdims=False)
        masked, own, send1, send2 = call(
            first_kernel,
            (vmem(BLK, 17 * BLK), vmem(17, BLK, BLK), vmem(k1, BLK, BLK), vmem(4, k2, BLK, BLK)), 1, 1,
        )(pattern, density)
        got1 = send(send1, "zh")
        x = spread(send2)
        send_s = call(functools.partial(gather_kernel, 2, starts[0]), vmem(ks, BLK, BLK), 1, 2)(table, own, x)
        got1, send_s, x = lax.optimization_barrier((got1, send_s, x))
        got_s, got_c = send(send_s, "seam"), send(x, "c")
        own, x, got_c = lax.optimization_barrier((own, x, got_c))
        send_a, edge = call(
            functools.partial(third_kernel, nzl, starts[1]), (vmem(ka, BLK, BLK), vmem(k1, BLK, BLK)), 1, 4,
        )(table, own, x, send1, got1)
        got_a = send(send_a, "z")
        got_f, got_w = send(edge, "far"), send(edge, "wide")
        w = spread(jnp.broadcast_to(got1, (4, k1, BLK, BLK)))
        w, got_s = lax.optimization_barrier((w, got_s))
        send_b = call(functools.partial(gather_kernel, 4, starts[2]), vmem(kb, BLK, BLK), 1, 4)(table, own, x, w, got_c)
        got_b, got_d = send(send_b, "z"), send(w, "c")
        first = [own, x, w, got_c, got_s, got_a]
        pool = call(functools.partial(early_kernel, starts[3]), vmem(DUMMY, BLK, BLK), 1, len(first))(table, *first)
        late = starts[3] + sum(q.shape[0] for q in first)
        purified, _ = pl.pallas_call(
            functools.partial(final_kernel, late),
            out_shape=(vmem(1, BLK, KEPT * BLK, dtype=jnp.float32), vmem(DUMMY, BLK, BLK)),
            in_specs=[scalars()] * 2 + [whole()] * 6,
            out_specs=(whole(), whole()),
            scratch_shapes=[pltpu.VMEM((BLK, KEPT * BLK), jnp.float32), pltpu.VMEM((BLK, KEPT * BLK), jnp.bfloat16)],
            input_output_aliases={7: 1},
            compiler_params=pltpu.CompilerParams(vmem_limit_bytes=10 << 20),
        )(table, keep, masked, got_d, got_b, got_f, got_w, pool)
        return purified

    return jax.shard_map(
        body,
        mesh=fine,
        in_specs=(P(AXES, None, None), P(AXES, None), P(AXES, None)),
        out_specs=P(AXES, None, None),
        check_vma=False,
    )
```

```python
import functools

import jax
import jax.numpy as jnp
import numpy as np
from jax import lax
from jax.experimental import pallas as pl
from jax.experimental.pallas import tpu as pltpu
from jax.sharding import Mesh, PartitionSpec as P

BLK = 128
BAND_HALF = 8
KEEP_HALF = 10
KEPT = 21
AXES = ("y", "zl", "c", "zh", "x")
UPPER = BAND_HALF + 1
DUMMY = KEPT * UPPER


def canonical(row, offset, n):
    return (row % n, offset) if offset >= 0 else ((row + offset) % n, -offset)


def own_lists(p):
    return list(range(0, 4 - p)) + list(range(8 - p, 9)), list(range(-p - 4, -p)) + list(range(4 - p, 8 - p))


def make_plan(ny, nzl):
    n = ny * nzl * 16

    def place(y, zl, c, zh, x):
        return (((y % ny) * nzl + zl) * 2 + c) * 8 + zh * 4 + x % 4

    coords = [(y, zl, c, zh, x) for y in range(ny) for zl in range(nzl) for c in range(2) for zh in range(2) for x in range(4)]

    def ring(y, zl, zh, step):
        z = zh * nzl + zl
        y += 1 if (step == 1 and zl == nzl - 1) else -1 if (step == -1 and zl == 0) else 0
        z = (z + step) % (2 * nzl)
        return y, z % nzl, z // nzl

    def pad(blocks, k):
        return list(blocks) + [None] * (k - len(blocks))

    need = [{((i - KEEP_HALF + u) % n, o): u * UPPER + o for u in range(KEPT) for o in range(UPPER) if u + o < KEPT} for i in range(n)]
    lists = [own_lists(x) for y, zl, c, zh, x in coords]
    own = [[canonical(i, o, n) for o in range(-8, 9)] for i in range(n)]
    sent1 = [[canonical(i, o, n) for o in same] for i, (same, _) in enumerate(lists)]
    sent2 = [[canonical(i, o, n) for o in same + mixed] for i, (same, mixed) in enumerate(lists)]
    moves = {}
    moves["zh"] = [(i, place(y, zl, c, 1 - zh, x)) for i, (y, zl, c, zh, x) in enumerate(coords)]
    moves["c"] = [(i, place(y, zl, 1 - c, zh, x)) for i, (y, zl, c, zh, x) in enumerate(coords)]
    moves["seam"], moves["z"], moves["far"] = [], [], []
    for i, (y, zl, c, zh, x) in enumerate(coords):
        if (zl, c, zh) in ((0, 0, 0), (nzl - 1, 1, 1)):
            moves["seam"].append((i, place(y, zl, c, 1 - zh, x)))
        if (zl, c, zh) == (nzl - 1, 0, 1):
            moves["seam"].append((i, place(y + 1, 0, 0, 0, x)))
        y2, zl2, zh2 = ring(y, zl, zh, 1 if c else -1)
        moves["z"].append((i, place(y2, zl2, 1 - c, zh2, x)))
        for step in (1, -1):
            y2, zl2, zh2 = ring(y, zl, zh, step)
            if (zh2 == 0 and x < 2 and step == 1) or (zh2 == 1 and x >= 2 and step == -1):
                moves["far"].append((i, place(y2, zl2, c, zh2, x)))

    def moved(sends, name):
        got = [[None] * len(sends[0]) for _ in range(n)]
        for s, d in moves[name]:
            got[d] = sends[s]
        return got

    def join(*parts):
        return [sum(row, []) for row in zip(*parts)]

    got1 = moved(sent1, "zh")
    got2 = [[sum([sent2[i - i % 4 + q] for q in range(4)], []) for i in range(n)]]
    got3 = [[sum([got1[i - i % 4 + q] for q in range(4)], []) for i in range(n)]]
    stock2 = join(own, *got2)
    stock3 = join(stock2, *got3)
    got_c = moved(join(*got2), "c")
    got_d = moved(join(*got3), "c")
    stock4 = join(stock3, got_c)
    known = [set(row) for row in join(stock4, got_d)]

    def choose(name, stock):
        sends = [[] for _ in range(n)]
        for s, d in moves[name]:
            sends[s] = [b for b in need[d] if b not in known[d] and b in set(stock[s])]
        k = max(map(len, sends))
        sends = [pad(q, k) for q in sends]
        got = moved(sends, name)
        for d in range(n):
            known[d] |= set(got[d])
        return sends, got

    sent_s, got_s = choose("seam", stock2)
    sent_a, got_a = choose("z", stock2)
    sent_b, got_b = choose("z", stock4)
    sent_f, got_f = choose("far", stock4)
    assert all(set(need[d]) <= known[d] for d in range(n))

    def where(sends, stock):
        return np.array([[src.index(b) if b is not None else 0 for b in q] for q, src in zip(sends, stock)], np.int32)

    sent_s, got_s = [pad(q, 24) for q in sent_s], [pad(q, 24) for q in got_s]
    arrived = join(stock4, got_s, got_a, got_d, got_b, got_f)
    spots = np.full((n, len(arrived[0])), DUMMY, np.int32)
    for i in range(n):
        seen = set()
        for k, b in enumerate(arrived[i]):
            if b in need[i] and b not in seen:
                seen.add(b)
                spots[i, k] = need[i][b]
    parts = [where(sent_s, stock2), where(sent_a, stock2), where(sent_b, stock4), where(sent_f, stock4), spots]
    starts = np.cumsum([0] + [q.shape[1] for q in parts])
    sizes = [len(lists[0][0]), len(sent2[0])] + [q.shape[1] for q in parts]
    return moves, np.concatenate(parts, axis=1), sizes, [int(q) for q in starts]


def vmem(*shape, dtype=jnp.bfloat16):
    return jax.ShapeDtypeStruct(shape, dtype)


def whole():
    return pl.BlockSpec(memory_space=pltpu.VMEM)


def scalars():
    return pl.BlockSpec(memory_space=pltpu.SMEM)


def call(kernel, outs, n_scalar, n_vector, scratch=(), mib=8):
    return pl.pallas_call(
        kernel,
        out_shape=outs,
        in_specs=[scalars()] * n_scalar + [whole()] * n_vector,
        out_specs=jax.tree.map(lambda _: whole(), outs),
        scratch_shapes=scratch,
        compiler_params=pltpu.CompilerParams(vmem_limit_bytes=mib << 20),
    )


def first_kernel(pattern, strip, masked, own, send1, send2):
    for slot in range(2 * BAND_HALF + 1):
        cols = slice(slot * BLK, (slot + 1) * BLK)
        block = strip[0, :, cols] * pattern[0, slot].astype(jnp.bfloat16)
        masked[:, cols] = block
        own[slot] = block if slot >= BAND_HALF else block.T
    p = lax.axis_index("x")
    for k in range(send2.shape[1]):
        if k < 5:
            offset = jnp.where(k < 4 - p, k, k + 4)
            send1[k] = own[BAND_HALF + offset]
        else:
            offset = k - 9 - p if k < 9 else k - 5 - p
        block = own[BAND_HALF + offset]
        for peer in range(4):
            send2[peer, k] = block


def gather(start, table, sources, outs):
    for out in outs:

        def pack(k, carry, out=out, start=start):
            at = table[start + k]
            low = 0
            for source in sources:
                count = source.shape[0]

                @pl.when((at >= low) & (at < low + count))
                def _(source=source, low=low):
                    out[k] = source[at - low]

                low += count
            return carry

        lax.fori_loop(0, out.shape[0], pack, 0)
        start += out.shape[0]


def gather_kernel(n_sources, start, table, *refs):
    gather(start, table, refs[:n_sources], refs[n_sources:])


def product(left, first, pool, v, width):
    last = KEPT - 1 - first
    blank = jnp.zeros((BLK, BLK), jnp.bfloat16)
    total = None
    for upper in (True, False):

        def block(u, col):
            row, offset = (u, col - u) if upper else (col, u - col)
            return pool[row * UPPER + offset] if (0 if upper else 1) <= offset <= BAND_HALF else blank

        low, high = (v - BAND_HALF, v + width - 1) if upper else (v + 1, v + width - 1 + BAND_HALF)
        low, high = max(first, low), min(last, high)
        if low > high:
            continue
        across = [
            jnp.concatenate([block(u, col) for u in range(low, high + 1)], axis=0 if upper else 1)
            for col in range(v, v + width)
        ]
        part = lax.dot_general(
            left[:, (low - first) * BLK : (high - first + 1) * BLK],
            jnp.concatenate(across, axis=1 if upper else 0),
            (((1,), (0 if upper else 1,)), ((), ())),
            preferred_element_type=jnp.float32,
        )
        total = part if total is None else total + part
    return total


def flags(keep, v, width):
    return jnp.concatenate([jnp.full((1, BLK), keep[0, v + j].astype(jnp.float32)) for j in range(width)], axis=1)


def place(low, spots, sources, pool):
    for source in sources:

        def put(k, carry, source=source, low=low):
            at = spots[low + k]

            @pl.when(at < DUMMY)
            def _():
                pool[at] = source[k]

            return carry

        lax.fori_loop(0, source.shape[0], put, 0)
        low += source.shape[0]


def early_kernel(start, spots, *refs):
    place(start, spots, refs[:-1], refs[-1])


def final_kernel(start, spots, keep, masked, *refs):
    *sources, _, out, pool, square, rounded = refs
    place(start, spots, sources, pool)
    groups = [(v, min(2, KEPT - v)) for v in range(0, KEPT, 2)]
    for v, width in groups:
        cols = slice(v * BLK, (v + width) * BLK)
        value = product(masked, KEEP_HALF - BAND_HALF, pool, v, width) * flags(keep, v, width)
        square[:, cols] = value
        rounded[:, cols] = value.astype(jnp.bfloat16)
    for v, width in groups:
        cols = slice(v * BLK, (v + width) * BLK)
        flag = flags(keep, v, width)
        cube = flag * product(rounded, 0, pool, v, width)
        out[0, :, cols] = flag * (3.0 * square[:, cols] - 2.0 * cube)


def solution(mesh):
    ny, nzl = mesh.shape["row"], mesh.shape["col"] // 2
    moves, tables, counts, starts = make_plan(ny, nzl)
    k1, k2, ks, ka, kb, kf, _ = counts
    fine = Mesh(mesh.devices.reshape(ny, nzl, 2, 2, 4), AXES)

    def send(array, name):
        return lax.ppermute(array, AXES, moves[name])

    def spread(copies):
        return lax.all_to_all(copies, "x", 0, 0).reshape(-1, BLK, BLK)

    def body(density, pattern, keep):
        table = lax.dynamic_index_in_dim(jnp.asarray(tables), lax.axis_index(AXES), 0, keepdims=False)
        masked, own, send1, send2 = call(
            first_kernel,
            (vmem(BLK, 17 * BLK), vmem(17, BLK, BLK), vmem(k1, BLK, BLK), vmem(4, k2, BLK, BLK)), 1, 1,
        )(pattern, density)
        got1 = send(send1, "zh")
        x = spread(send2)
        send_s = call(functools.partial(gather_kernel, 2, starts[0]), vmem(ks, BLK, BLK), 1, 2)(table, own, x)
        got1, send_s, x = lax.optimization_barrier((got1, send_s, x))
        got_s, got_c = send(send_s, "seam"), send(x, "c")
        send_a = call(functools.partial(gather_kernel, 2, starts[1]), vmem(ka, BLK, BLK), 1, 2)(table, own, x)
        got_a = send(send_a, "z")
        w = spread(jnp.broadcast_to(got1, (4, k1, BLK, BLK)))
        w, got_s, got_c = lax.optimization_barrier((w, got_s, got_c))
        send_b, send_f = call(
            functools.partial(gather_kernel, 4, starts[2]), (vmem(kb, BLK, BLK), vmem(kf, BLK, BLK)), 1, 4,
        )(table, own, x, w, got_c)
        got_b, got_f, got_d = send(send_b, "z"), send(send_f, "far"), send(w, "c")
        first = [own, x, w, got_c, got_s, got_a]
        pool = call(functools.partial(early_kernel, starts[4]), vmem(DUMMY, BLK, BLK), 1, len(first))(table, *first)
        late = starts[4] + sum(q.shape[0] for q in first)
        purified, _ = pl.pallas_call(
            functools.partial(final_kernel, late),
            out_shape=(vmem(1, BLK, KEPT * BLK, dtype=jnp.float32), vmem(DUMMY, BLK, BLK)),
            in_specs=[scalars()] * 2 + [whole()] * 5,
            out_specs=(whole(), whole()),
            scratch_shapes=[pltpu.VMEM((BLK, KEPT * BLK), jnp.float32), pltpu.VMEM((BLK, KEPT * BLK), jnp.bfloat16)],
            input_output_aliases={6: 1},
            compiler_params=pltpu.CompilerParams(vmem_limit_bytes=24 << 20),
        )(table, keep, masked, got_d, got_b, got_f, pool)
        return purified

    return jax.shard_map(
        body,
        mesh=fine,
        in_specs=(P(AXES, None, None), P(AXES, None), P(AXES, None)),
        out_specs=P(AXES, None, None),
        check_vma=False,
    )
```

```python
import functools

import jax
import jax.numpy as jnp
import numpy as np
from jax import lax
from jax.experimental import pallas as pl
from jax.experimental.pallas import tpu as pltpu
from jax.sharding import Mesh, PartitionSpec as P

BLK = 128
BAND_HALF = 8
KEEP_HALF = 10
KEPT = 21
AXES = ("y", "zl", "c", "zh", "x")
UPPER = BAND_HALF + 1
DUMMY = KEPT * UPPER


def canonical(row, offset, n):
    return (row % n, offset) if offset >= 0 else ((row + offset) % n, -offset)


def own_lists(p):
    return list(range(0, 4 - p)) + list(range(8 - p, 9)), list(range(-p - 4, -p)) + list(range(4 - p, 8 - p))


def make_plan(ny, nzl):
    n = ny * nzl * 16

    def place(y, zl, c, zh, x):
        return (((y % ny) * nzl + zl) * 2 + c) * 8 + zh * 4 + x % 4

    coords = [(y, zl, c, zh, x) for y in range(ny) for zl in range(nzl) for c in range(2) for zh in range(2) for x in range(4)]

    def ring(y, zl, zh, step):
        z = zh * nzl + zl
        y += 1 if (step == 1 and zl == nzl - 1) else -1 if (step == -1 and zl == 0) else 0
        z = (z + step) % (2 * nzl)
        return y, z % nzl, z // nzl

    def pad(blocks, k):
        return list(blocks) + [None] * (k - len(blocks))

    need = [{((i - KEEP_HALF + u) % n, o): u * UPPER + o for u in range(KEPT) for o in range(UPPER) if u + o < KEPT} for i in range(n)]
    lists = [own_lists(x) for y, zl, c, zh, x in coords]
    own = [[canonical(i, o, n) for o in range(-8, 9)] for i in range(n)]
    sent1 = [[canonical(i, o, n) for o in same] for i, (same, _) in enumerate(lists)]
    sent2 = [[canonical(i, o, n) for o in same + mixed] for i, (same, mixed) in enumerate(lists)]
    moves = {}
    moves["zh"] = [(i, place(y, zl, c, 1 - zh, x)) for i, (y, zl, c, zh, x) in enumerate(coords)]
    moves["c"] = [(i, place(y, zl, 1 - c, zh, x)) for i, (y, zl, c, zh, x) in enumerate(coords)]
    moves["seam"], moves["z"], moves["far"] = [], [], []
    for i, (y, zl, c, zh, x) in enumerate(coords):
        if (zl, c, zh) in ((0, 0, 0), (nzl - 1, 1, 1)):
            moves["seam"].append((i, place(y, zl, c, 1 - zh, x)))
        if (zl, c, zh) == (nzl - 1, 0, 1):
            moves["seam"].append((i, place(y + 1, 0, 0, 0, x)))
        y2, zl2, zh2 = ring(y, zl, zh, 1 if c else -1)
        moves["z"].append((i, place(y2, zl2, 1 - c, zh2, x)))
        for step in (1, -1):
            y2, zl2, zh2 = ring(y, zl, zh, step)
            if (zh2 == 0 and x < 2 and step == 1) or (zh2 == 1 and x >= 2 and step == -1):
                moves["far"].append((i, place(y2, zl2, c, zh2, x)))

    def moved(sends, name):
        got = [[None] * len(sends[0]) for _ in range(n)]
        for s, d in moves[name]:
            got[d] = sends[s]
        return got

    def join(*parts):
        return [sum(row, []) for row in zip(*parts)]

    got1 = moved(sent1, "zh")
    got2 = [[sum([sent2[i - i % 4 + q] for q in range(4)], []) for i in range(n)]]
    got3 = [[sum([got1[i - i % 4 + q] for q in range(4)], []) for i in range(n)]]
    stock2 = join(own, *got2)
    stock3 = join(stock2, *got3)
    got_c = moved(join(*got2), "c")
    got_d = moved(join(*got3), "c")
    stock4 = join(stock3, got_c)
    known = [set(row) for row in join(stock4, got_d)]

    def choose(name, stock):
        sends = [[] for _ in range(n)]
        for s, d in moves[name]:
            sends[s] = [b for b in need[d] if b not in known[d] and b in set(stock[s])]
        k = max(map(len, sends))
        sends = [pad(q, k) for q in sends]
        got = moved(sends, name)
        for d in range(n):
            known[d] |= set(got[d])
        return sends, got

    sent_s, got_s = choose("seam", stock2)
    sent_a, got_a = choose("z", stock2)
    sent_b, got_b = choose("z", stock4)
    sent_f, got_f = choose("far", stock4)
    assert all(set(need[d]) <= known[d] for d in range(n))

    def where(sends, stock):
        return np.array([[src.index(b) if b is not None else 0 for b in q] for q, src in zip(sends, stock)], np.int32)

    sent_s, got_s = [pad(q, 24) for q in sent_s], [pad(q, 24) for q in got_s]
    arrived = join(stock4, got_s, got_a, got_d, got_b, got_f)
    spots = np.full((n, len(arrived[0])), DUMMY, np.int32)
    for i in range(n):
        seen = set()
        for k, b in enumerate(arrived[i]):
            if b in need[i] and b not in seen:
                seen.add(b)
                spots[i, k] = need[i][b]
    parts = [where(sent_s, stock2), where(sent_a, stock2), where(sent_b, stock4), where(sent_f, stock4), spots]
    starts = np.cumsum([0] + [q.shape[1] for q in parts])
    sizes = [len(lists[0][0]), len(sent2[0])] + [q.shape[1] for q in parts]
    return moves, np.concatenate(parts, axis=1), sizes, [int(q) for q in starts]


def vmem(*shape, dtype=jnp.bfloat16):
    return jax.ShapeDtypeStruct(shape, dtype)


def whole():
    return pl.BlockSpec(memory_space=pltpu.VMEM)


def scalars():
    return pl.BlockSpec(memory_space=pltpu.SMEM)


def call(kernel, outs, n_scalar, n_vector, scratch=(), mib=8):
    return pl.pallas_call(
        kernel,
        out_shape=outs,
        in_specs=[scalars()] * n_scalar + [whole()] * n_vector,
        out_specs=jax.tree.map(lambda _: whole(), outs),
        scratch_shapes=scratch,
        compiler_params=pltpu.CompilerParams(vmem_limit_bytes=mib << 20),
    )


def first_kernel(pattern, strip, masked, own, send1, send2):
    for slot in range(2 * BAND_HALF + 1):
        cols = slice(slot * BLK, (slot + 1) * BLK)
        block = strip[0, :, cols] * pattern[0, slot].astype(jnp.bfloat16)
        masked[:, cols] = block
        own[slot] = block if slot >= BAND_HALF else block.T
    p = lax.axis_index("x")
    for k in range(send2.shape[1]):
        if k < 5:
            offset = jnp.where(k < 4 - p, k, k + 4)
            send1[k] = own[BAND_HALF + offset]
        else:
            offset = k - 9 - p if k < 9 else k - 5 - p
        block = own[BAND_HALF + offset]
        for peer in range(4):
            send2[peer, k] = block


def gather(start, table, sources, outs):
    for out in outs:

        def pack(k, carry, out=out, start=start):
            at = table[start + k]
            low = 0
            for source in sources:
                count = source.shape[0]

                @pl.when((at >= low) & (at < low + count))
                def _(source=source, low=low):
                    out[k] = source[at - low]

                low += count
            return carry

        lax.fori_loop(0, out.shape[0], pack, 0)
        start += out.shape[0]


def gather_kernel(n_sources, start, table, *refs):
    gather(start, table, refs[:n_sources], refs[n_sources:])


def product(left, first, pool, v, width):
    last = KEPT - 1 - first
    blank = jnp.zeros((BLK, BLK), jnp.bfloat16)
    total = None
    for upper in (True, False):

        def block(u, col):
            row, offset = (u, col - u) if upper else (col, u - col)
            return pool[row * UPPER + offset] if (0 if upper else 1) <= offset <= BAND_HALF else blank

        low, high = (v - BAND_HALF, v + width - 1) if upper else (v + 1, v + width - 1 + BAND_HALF)
        low, high = max(first, low), min(last, high)
        if low > high:
            continue
        across = [
            jnp.concatenate([block(u, col) for u in range(low, high + 1)], axis=0 if upper else 1)
            for col in range(v, v + width)
        ]
        part = lax.dot_general(
            left[:, (low - first) * BLK : (high - first + 1) * BLK],
            jnp.concatenate(across, axis=1 if upper else 0),
            (((1,), (0 if upper else 1,)), ((), ())),
            preferred_element_type=jnp.float32,
        )
        total = part if total is None else total + part
    return total


def flags(keep, v, width):
    return jnp.concatenate([jnp.full((1, BLK), keep[0, v + j].astype(jnp.float32)) for j in range(width)], axis=1)


def place(low, spots, sources, pool):
    for source in sources:

        def put(k, carry, source=source, low=low):
            pool[spots[low + k]] = source[k]
            return carry

        lax.fori_loop(0, source.shape[0], put, 0, unroll=True)
        low += source.shape[0]


def early_kernel(start, spots, *refs):
    place(start, spots, refs[:-1], refs[-1])


def final_kernel(start, spots, keep, masked, *refs):
    *sources, _, out, pool, square, rounded = refs
    place(start, spots, sources, pool)
    groups = [(v, min(2, KEPT - v)) for v in range(0, KEPT, 2)]
    for v, width in groups:
        cols = slice(v * BLK, (v + width) * BLK)
        value = product(masked, KEEP_HALF - BAND_HALF, pool, v, width) * flags(keep, v, width)
        square[:, cols] = value
        rounded[:, cols] = value.astype(jnp.bfloat16)
    for v, width in groups:
        cols = slice(v * BLK, (v + width) * BLK)
        flag = flags(keep, v, width)
        cube = flag * product(rounded, 0, pool, v, width)
        out[0, :, cols] = flag * (3.0 * square[:, cols] - 2.0 * cube)


def solution(mesh):
    ny, nzl = mesh.shape["row"], mesh.shape["col"] // 2
    moves, tables, counts, starts = make_plan(ny, nzl)
    k1, k2, ks, ka, kb, kf, _ = counts
    fine = Mesh(mesh.devices.reshape(ny, nzl, 2, 2, 4), AXES)

    def send(array, name):
        return lax.ppermute(array, AXES, moves[name])

    def spread(copies):
        return lax.all_to_all(copies, "x", 0, 0).reshape(-1, BLK, BLK)

    def body(density, pattern, keep):
        table = lax.dynamic_index_in_dim(jnp.asarray(tables), lax.axis_index(AXES), 0, keepdims=False)
        masked, own, send1, send2 = call(
            first_kernel,
            (vmem(BLK, 17 * BLK), vmem(17, BLK, BLK), vmem(k1, BLK, BLK), vmem(4, k2, BLK, BLK)), 1, 1,
        )(pattern, density)
        got1 = send(send1, "zh")
        x = spread(send2)
        send_s = call(functools.partial(gather_kernel, 2, starts[0]), vmem(ks, BLK, BLK), 1, 2)(table, own, x)
        got1, send_s, x = lax.optimization_barrier((got1, send_s, x))
        got_s, got_c = send(send_s, "seam"), send(x, "c")
        send_a = call(functools.partial(gather_kernel, 2, starts[1]), vmem(ka, BLK, BLK), 1, 2)(table, own, x)
        got_a = send(send_a, "z")
        w = spread(jnp.broadcast_to(got1, (4, k1, BLK, BLK)))
        w, got_s, got_c = lax.optimization_barrier((w, got_s, got_c))
        send_b, send_f = call(
            functools.partial(gather_kernel, 4, starts[2]), (vmem(kb, BLK, BLK), vmem(kf, BLK, BLK)), 1, 4,
        )(table, own, x, w, got_c)
        got_b, got_f, got_d = send(send_b, "z"), send(send_f, "far"), send(w, "c")
        first = [own, x, w, got_c, got_s, got_a]
        pool = call(functools.partial(early_kernel, starts[4]), vmem(DUMMY + 1, BLK, BLK), 1, len(first))(table, *first)
        late = starts[4] + sum(q.shape[0] for q in first)
        purified, _ = pl.pallas_call(
            functools.partial(final_kernel, late),
            out_shape=(vmem(1, BLK, KEPT * BLK, dtype=jnp.float32), vmem(DUMMY + 1, BLK, BLK)),
            in_specs=[scalars()] * 2 + [whole()] * 5,
            out_specs=(whole(), whole()),
            scratch_shapes=[pltpu.VMEM((BLK, KEPT * BLK), jnp.float32), pltpu.VMEM((BLK, KEPT * BLK), jnp.bfloat16)],
            input_output_aliases={6: 1},
            compiler_params=pltpu.CompilerParams(vmem_limit_bytes=24 << 20),
        )(table, keep, masked, got_d, got_b, got_f, pool)
        return purified

    return jax.shard_map(
        body,
        mesh=fine,
        in_specs=(P(AXES, None, None), P(AXES, None), P(AXES, None)),
        out_specs=P(AXES, None, None),
        check_vma=False,
    )
```
